32 devices in a mesh: expert: 8 (over y, x, core), tensor: 4 (over z).
Axes of the slice: x: 2, y: 2, z: 4, core: 2. Of those that a mesh axis runs over, the one named last changes fastest.
Arguments:
- residual: bfloat16 [512, 7168], P('expert', 'tensor'), may hold values from -40 to 40
- attn_parts: bfloat16 [4, 512, 7168], P('tensor', 'expert'), may hold values from -2 to 2
- norm_gain: bfloat16 [7168], P('tensor'), may hold values from 0.099609375 to 1.8984375
- routes: int32 [512, 2], P('expert'), may hold values from 0 to 7, all different within a row; in each aligned block of 64 rows (0 to 63, 64 to 127, ...) at most 24 rows name the same one
- route_weights: float32 [512, 2], P('expert'), may hold values from 0.05 to 0.6
- w_gate: bfloat16 [8, 7168, 2048], P('expert', None, 'tensor'), may hold values from -0.06023809 to 0.06023809
- w_gate_q: bfloat16 [8, 7168, 2048], P('expert', None, 'tensor'), may hold values from -0.09567226 to 0.09567226
Outputs:
- token_error: float32 [512], P('expert')
- expert_error: float32 [8], P('expert')
- hess_diag: float32 [8, 7168], P('expert', 'tensor')
The draws below stay inside these ranges and needn't reach their ends.
Inputs may be any that keep to these rules, and one draw needn't show every extreme that they name: `routes`: no expert is named by more than 24 of the rows of one device, and in every draw some expert is named by exactly 24 of them; the 2 experts of a token are distinct; every expert is named by some token.
All inputs are finite; a program needn't handle non-finite values.
Results may differ from the reference program's by a relative error of at most 0.0023.
Values may be sent and summed in bfloat16 or wider, within the bound.
No kernel may reach another device: no remote copies, remote signals or barrier semaphores. Data moves between devices by JAX's collectives and lax.ppermute only.
A program may use at most 64 MiB of HBM per device.

```python
import math
import jax
import jax.numpy as jnp
import numpy as np
from jax import lax

D = 7168
FF = 2048
QGROUP = 128
TOK_DEV = 64
TOKENS = 512
EXPERTS = 8
TOPK = 2
CAP = 24
N_EXPERT = 8
N_TENSOR = 4


def weight_pair(key):
    base_key = jax.random.fold_in(key, 7301)
    weight_scale = 1.0 / math.sqrt(D)

    def one_expert(expert_id):
        expert_key = jax.random.fold_in(base_key, expert_id)
        key_list = jax.random.split(expert_key, 4)
        base_values = jnp.clip(jax.random.normal(key_list[0], (D, FF), jnp.float32), -5.0, 5.0)
        group_scale = jnp.exp(jax.random.uniform(key_list[1], (D // QGROUP, FF), jnp.float32, math.log(0.1), 0.0))
        group_scale = jnp.repeat(group_scale, QGROUP, axis=0)
        column_scale = jnp.exp(jax.random.uniform(key_list[2], (1, FF), jnp.float32, math.log(0.3), math.log(3.0)))
        noise_values = jax.random.uniform(key_list[3], (D, FF), jnp.float32, -1.0, 1.0)
        full_values = base_values * weight_scale
        quant_values = full_values + weight_scale * group_scale * column_scale * noise_values
        return (full_values.astype(jnp.bfloat16), quant_values.astype(jnp.bfloat16))
    return lax.map(one_expert, jnp.arange(EXPERTS, dtype=jnp.int32))


def draw_w_gate(key, part):
    return weight_pair(key)[0]


def draw_w_gate_q(key, part):
    return weight_pair(key)[1]


def draw_residual(key, part):
    key_list = jax.random.split(jax.random.fold_in(key, 4409), 2)
    column = jnp.arange(D, dtype=jnp.float32)[None, :] / (D - 1)
    roughness = jnp.exp(jax.random.uniform(key_list[1], (TOKENS, D), jnp.float32, math.log(0.5), math.log(2.0)))
    ramp_scale = jnp.sqrt(1.0 + 2.0 * column)
    base_values = jnp.clip(jax.random.normal(key_list[0], (TOKENS, D), jnp.float32), -5.0, 5.0)
    return jnp.clip(base_values * ramp_scale * roughness, -40.0, 40.0).astype(jnp.bfloat16)


def spiked(entries, key, source, target, shards_of, factor):
    owner, partner = [(jnp.arange(entries.shape[axis_at]) // (entries.shape[axis_at] // shards_of)).reshape([-1 if axis == axis_at else 1 for axis in range(entries.ndim)]) for axis_at in (source, target)]
    chosen = jax.random.permutation(key, shards_of)[partner]
    strong = (owner == chosen) | (owner == (partner + shards_of // 2) % shards_of)
    return jnp.where(strong, factor * entries, entries)


def block_scale(key, dims, pieces, smallest, largest):
    gain, own = 1.0, jax.random.fold_in(key, 6)
    for dim, parts in pieces:
        steps = jnp.exp(jax.random.uniform(jax.random.fold_in(own, dim), (parts,), jnp.float32, smallest / len(pieces), largest / len(pieces)))
        gain = gain * jnp.repeat(steps, dims[dim] // parts).reshape([-1 if axis == dim else 1 for axis in range(len(dims))])
    return gain


def shared_out(own_key, own, number, rows, count, top, limit, slope):
    sequence = jax.random.permutation(own_key, count)
    heavy_load, common = shares(count, rows * top, limit, slope, True), shares(count, rows * top, limit, slope, False)
    places = jnp.arange(count)

    def named(tallies, rotation):
        used = int((tallies > 0).sum())
        fixed = max(1, used // 4)
        shifted = fixed + (places - fixed + rotation * (used - fixed)) % max(1, count - fixed)
        return jnp.zeros((count,), jnp.int32).at[sequence[jnp.where(places < fixed, places, shifted)]].set(jnp.asarray(tallies, jnp.int32))

    tallies = jnp.where(number % 4 == 0, named(heavy_load, number // 4), named(common, number - number // 4 - 1))
    mixed = jax.random.permutation(jax.random.fold_in(own, 3), count)
    source_of, taker = mixed[0:count // 2 * 2:2], mixed[1:count // 2 * 2:2]
    slack = jnp.minimum(tallies[source_of] - 1, limit - tallies[taker]) // 2
    slack = jnp.where((source_of == sequence[0]) | (taker == sequence[0]) | (tallies[taker] == 0), 0, jnp.maximum(slack, 0))
    shifted = jax.random.randint(jax.random.fold_in(own, 4), (count // 2,), 0, 1 << 20) % (slack + 1)
    tallies = tallies.at[source_of].add(-shifted).at[taker].add(shifted)
    labels = jnp.searchsorted(jnp.cumsum(tallies), jnp.arange(rows * top), side="right").astype(jnp.int32)
    table = labels.reshape(top, rows).T
    table = table[jax.random.permutation(jax.random.fold_in(own, 1), rows)]
    rotation = jax.random.randint(jax.random.fold_in(own, 2), (rows, 1), 0, top)
    return jnp.take_along_axis(table, (jnp.arange(top)[None, :] + rotation) % top, axis=1)


def shares(number_of, total, reach, slope, full):
    portions = [(1 << 20) // math.isqrt(rank ** slope) + 1 for rank in range(1, number_of + 1)]
    largest = reach if full else min(reach, max(-(-total // number_of), total * portions[0] // sum(portions)))
    least = 1 if total - largest >= number_of - 1 else 0
    given, rest = [largest] + [least] * (number_of - 1), total - largest - least * (number_of - 1)
    while rest > 0:
        movable = [i for i in range(1, number_of) if given[i] < largest] or [i for i in range(1, number_of) if given[i] < reach]
        whole, left = sum([portions[i] for i in movable]), rest
        for i in movable:
            more = min(reach - given[i], max(1, left * portions[i] // whole), rest)
            given[i] = given[i] + more
            rest = rest - more
    return np.array(given)


def noise_with(key, dims, deviation, most, shards, heavy, kind=jnp.bfloat16):
    values = deviation * jax.random.normal(key, dims, jnp.float32)
    if shards:
        values = values * block_scale(key, dims, shards, -0.22, 0.18)
    return jnp.clip(spiked(values, jax.random.fold_in(key, 3), *heavy), -most, most).astype(kind)


def setup_inputs(seed: int = 0) -> dict:
    seeds = jax.random.split(jax.random.key(seed), 8)
    residual = draw_residual(jax.random.fold_in(seeds[7], 71), 0)
    attn_parts = noise_with(seeds[1], (N_TENSOR, TOKENS, D), 0.25, 2.0, ((0, 4), (1, 8)), (0, 2, 4, 2.0))
    norm_gain = jnp.clip(1.0 + 0.18 * jax.random.normal(seeds[2], (D,), jnp.float32), 0.099609375, 1.8984375).astype(jnp.bfloat16)
    routes_keys = jax.random.split(jax.random.fold_in(seeds[3], 1), TOKENS // TOK_DEV)
    routes_turns = jax.random.permutation(jax.random.fold_in(seeds[3], 3), TOKENS // TOK_DEV)
    routes = jax.vmap(lambda own, number: shared_out(jax.random.fold_in(seeds[3], 2), own, number, TOK_DEV, EXPERTS, TOPK, CAP, 2))(routes_keys, routes_turns).reshape((TOKENS, TOPK))
    route_weights = jnp.clip(0.05 + 0.55 * jax.random.uniform(seeds[4], (TOKENS, TOPK), jnp.float32) ** block_scale(seeds[4], (TOKENS, TOPK), ((0, 8),), -0.2, 0.2), 0.05, 0.6)
    w_gate = draw_w_gate(jax.random.fold_in(seeds[7], 71), 0)
    w_gate_q = draw_w_gate_q(jax.random.fold_in(seeds[7], 71), 0)
    return {"residual": residual, "attn_parts": attn_parts, "norm_gain": norm_gain, "routes": routes, "route_weights": route_weights, "w_gate": w_gate, "w_gate_q": w_gate_q}


epsilon = 1e-06

def reference(residual, attn_parts, norm_gain, routes, route_weights, w_gate, w_gate_q):
    hidden = residual.astype(jnp.float32) + lax.optimization_barrier(jnp.sum(attn_parts.astype(jnp.float32), axis=0))
    mean_square = lax.optimization_barrier(jnp.mean(hidden * hidden, axis=1, keepdims=True))
    normed = (hidden * lax.rsqrt(mean_square + epsilon) * norm_gain.astype(jnp.float32)[None, :]).astype(jnp.bfloat16)
    flat_routes = routes.reshape(-1).astype(jnp.int32)
    route_total = TOKENS * TOPK
    most_rows = N_EXPERT * CAP

    def per_expert(expert_id):
        chosen = flat_routes == expert_id
        positions = jnp.nonzero(chosen, size=most_rows, fill_value=route_total)[0].astype(jnp.int32)
        valid = positions < route_total
        token_rows = jnp.minimum(positions // TOPK, TOKENS - 1).astype(jnp.int32)
        picked = jnp.where(valid[:, None], normed[token_rows], jnp.zeros((), jnp.bfloat16))
        full_out = jnp.dot(picked, w_gate[expert_id], preferred_element_type=jnp.float32)
        quant_out = jnp.dot(picked, w_gate_q[expert_id], preferred_element_type=jnp.float32)
        difference = full_out - quant_out
        route_err = lax.optimization_barrier(jnp.mean(difference * difference, axis=1))
        route_pow = lax.optimization_barrier(jnp.mean(full_out * full_out, axis=1))
        load_count = jnp.sum(chosen.astype(jnp.float32))
        picked_wide = picked.astype(jnp.float32)
        hess_row = 2.0 * lax.optimization_barrier(jnp.sum(picked_wide * picked_wide, axis=0)) / load_count
        return (positions, route_err, route_pow, hess_row)
    positions, route_err, route_pow, hess_diag = lax.map(per_expert, jnp.arange(EXPERTS, dtype=jnp.int32))
    expert_error = lax.optimization_barrier(jnp.sum(route_err, axis=1)) / (lax.optimization_barrier(jnp.sum(route_pow, axis=1)) + epsilon)
    flat_positions = positions.reshape(-1)
    err_all = jnp.zeros((route_total,), jnp.float32).at[flat_positions].set(route_err.reshape(-1), mode='drop')
    pow_all = jnp.zeros((route_total,), jnp.float32).at[flat_positions].set(route_pow.reshape(-1), mode='drop')
    ratios = (err_all / (pow_all + epsilon)).reshape(TOKENS, TOPK)
    token_error = lax.optimization_barrier(jnp.sum(route_weights * ratios, axis=1))
    return (token_error, expert_error, hess_diag)
```

```python
import jax
import jax.numpy as jnp
from jax import lax
from jax.experimental import pallas as pl
from jax.experimental.pallas import tpu as pltpu
from jax.sharding import PartitionSpec as P

D = 7168
FF = 2048
CAP = 24
EXTRA = 128


epsilon = 1e-06


def general_device(residual, attn_parts, norm_gain, routes, route_weights, w_gate, w_gate_q):
    n_expert = lax.axis_size("expert")
    tok_count = residual.shape[0]
    local_cols = residual.shape[1]
    top_count = routes.shape[1]
    gain_wide = norm_gain.astype(jnp.float32)[None, :]
    summed = lax.psum_scatter(
        attn_parts[0].astype(jnp.float32).astype(jnp.bfloat16),
        "tensor",
        scatter_dimension=1,
        tiled=True,
    ).astype(jnp.float32)
    hidden = residual.astype(jnp.float32) + summed
    squares = lax.psum(jnp.sum(hidden * hidden, axis=1), "tensor")
    scaling = lax.rsqrt(squares / D + epsilon)
    normed = (hidden * scaling[:, None] * gain_wide).astype(jnp.bfloat16)
    expert_ids = jnp.arange(n_expert, dtype=jnp.int32)
    flat_routes = routes.reshape(-1)
    one_hot = (flat_routes[:, None] == expert_ids[None, :]).astype(jnp.int32)
    earlier = jnp.cumsum(one_hot, axis=0) - one_hot
    slot_index = jnp.sum(earlier * one_hot, axis=1)
    target = flat_routes * CAP + slot_index
    load_counts = jnp.sum(one_hot, axis=0)
    slot_ids = jnp.arange(n_expert * CAP, dtype=jnp.int32)
    placing = (slot_ids[:, None] == target[None, :]).reshape(n_expert * CAP, tok_count, top_count)
    dispatch = jnp.sum(placing.astype(jnp.int32), axis=2).astype(jnp.bfloat16)
    count_send = load_counts.astype(jnp.bfloat16).reshape(n_expert, 1)
    outgoing = jnp.dot(dispatch, normed, preferred_element_type=jnp.float32).astype(jnp.bfloat16)
    outgoing = outgoing.reshape(n_expert, CAP, local_cols)
    arrived, arrived_counts = (
        lax.all_to_all(outgoing, "expert", split_axis=0, concat_axis=0, tiled=True),
        lax.all_to_all(count_send, "expert", split_axis=0, concat_axis=0, tiled=True),
    )
    own_block = arrived.reshape(n_expert * CAP, local_cols)
    column_block = lax.all_gather(own_block, "tensor", axis=1, tiled=True)
    full_acc = jnp.dot(column_block, w_gate[0], preferred_element_type=jnp.float32)
    quant_acc = jnp.dot(column_block, w_gate_q[0], preferred_element_type=jnp.float32)
    block_squares = jnp.einsum("rc,rc->c", own_block, own_block, preferred_element_type=jnp.float32)
    total_load = jnp.sum(arrived_counts.astype(jnp.float32))
    hess_local = 2.0 * block_squares / total_load
    difference = full_acc - quant_acc
    err_part = (jnp.sum(difference * difference, axis=1) / FF).reshape(n_expert, CAP)
    pow_part = (jnp.sum(full_acc * full_acc, axis=1) / FF).reshape(n_expert, CAP)
    err_slots, pow_slots = lax.psum((err_part, pow_part), "tensor")
    expert_total = jnp.sum(err_slots) / (jnp.sum(pow_slots) + epsilon)
    back_err, back_pow = (
        lax.all_to_all(err_slots, "expert", split_axis=0, concat_axis=0, tiled=True),
        lax.all_to_all(pow_slots, "expert", split_axis=0, concat_axis=0, tiled=True),
    )
    token_err = jnp.take(back_err.reshape(-1), target).reshape(tok_count, top_count)
    token_pow = jnp.take(back_pow.reshape(-1), target).reshape(tok_count, top_count)
    ratios = token_err / (token_pow + epsilon)
    token_error = jnp.sum(route_weights * ratios, axis=1)
    return (token_error, expert_total.reshape(1), hess_local.reshape(1, local_cols))


def product_kernel(first, last, *refs):
    it = iter(refs)
    expert_ref = next(it) if last else None
    near_ref, far_ref, w_ref, wq_ref = next(it), next(it), next(it), next(it)
    if not first:
        full_in, quant_in = next(it), next(it)
    if last:
        stats_ref, sums = next(it), next(it)
    else:
        full_out, quant_out = next(it), next(it)
    half = near_ref.shape[0]
    depth = w_ref.shape[0]
    step = pl.program_id(0)
    for part, ref in enumerate((near_ref, far_ref)):
        rows = slice(part * half, (part + 1) * half)
        x = ref[:, :depth]
        full = jnp.dot(x, w_ref[...], preferred_element_type=jnp.float32)
        quant = jnp.dot(x, wq_ref[...], preferred_element_type=jnp.float32)
        if not first:
            full = full + full_in[rows, :]
            quant = quant + quant_in[rows, :]
        if not last:
            full_out[rows, :] = full
            quant_out[rows, :] = quant
            continue
        diff = full - quant
        err = jnp.sum(diff * diff, axis=1, keepdims=True)
        power = jnp.sum(full * full, axis=1, keepdims=True)
        lane = lax.broadcasted_iota(jnp.int32, (half, EXTRA), 1)
        here = jnp.where(lane == 0, err, jnp.where(lane == 1, power, 0.0))

        @pl.when(step == 0)
        def _():
            sums[rows, :] = here

        @pl.when(step == pl.num_programs(0) - 1)
        def _():
            total = sums[rows, :] + here
            extra = ref[:, depth:].astype(jnp.float32)
            squares = extra[:, 0:1] + extra[:, 1:2] + extra[:, 2:3]
            scale = lax.rsqrt(squares / D + epsilon)
            scale = scale * scale
            mine = expert_ref[0].astype(jnp.float32)
            routed = jnp.sum(
                jnp.where((lane >= 3) & (extra == mine), 1.0, 0.0), axis=1, keepdims=True
            )
            out = jnp.where(
                lane < 2,
                total * (scale / FF),
                jnp.where(lane == 2, routed, jnp.where(lane == 3, scale * routed, 0.0)),
            )
            out = jnp.where((lane == 4) | (lane == 5), 0.0, out)
            stats_ref[:, rows] = out.T[:8, :]


def product(near, far, w, wq, number, depth, sums, expert, last):
    first = sums is None
    half = near.shape[0]
    rows = 2 * half
    cols = w.shape[2]
    tile = cols // 2
    whole = lambda j: (0, 0)
    slab = pl.BlockSpec((None, depth, tile), lambda j: (0, number, j))
    column = pl.BlockSpec((rows, tile), lambda j: (0, j))
    args, specs = [], []
    if last:
        args.append(expert)
        specs.append(pl.BlockSpec(memory_space=pltpu.SMEM))
    args += [near, far, w, wq]
    specs += [pl.BlockSpec(near.shape, whole), pl.BlockSpec(far.shape, whole), slab, slab]
    aliases = {}
    if not first:
        if not last:
            aliases = {len(args): 0, len(args) + 1: 1}
        args += list(sums)
        specs += [column, column]
    if last:
        out_shape = jax.ShapeDtypeStruct((8, rows), jnp.float32)
        out_specs = pl.BlockSpec((8, rows), whole)
        scratch = [pltpu.VMEM((rows, EXTRA), jnp.float32)]
    else:
        out_shape = [jax.ShapeDtypeStruct((rows, cols), jnp.float32)] * 2
        out_specs = [column, column]
        scratch = []

    def kernel(*refs):
        product_kernel(first, last, *refs)

    return pl.pallas_call(
        kernel,
        grid=(2,),
        in_specs=specs,
        out_specs=out_specs,
        out_shape=out_shape,
        scratch_shapes=scratch,
        input_output_aliases=aliases,
        compiler_params=pltpu.CompilerParams(vmem_limit_bytes=32 * 1024 * 1024),
        cost_estimate=pl.CostEstimate(
            flops=4 * rows * depth * cols, bytes_accessed=4 * depth * cols + 2 * rows * depth, transcendentals=0
        ),
    )(*args)


def line_device(residual, attn_parts, norm_gain, routes, route_weights, w_gate, w_gate_q):
    n_quarters = 4
    z = lax.axis_index("tensor")
    e = lax.axis_index("expert")
    tok = residual.shape[0]
    width = residual.shape[1]
    is_end = (z == 0) | (z == 3)
    low = z == 1
    own_residual = residual.astype(jnp.float32)

    def partial(k):
        return attn_parts[0][:, k * width : (k + 1) * width].astype(jnp.float32) + jnp.where(
            z == k, own_residual, 0.0
        )

    inward = [(0, 1), (3, 2)]
    outward = [(1, 0), (2, 3)]
    both = inward + outward
    middle = [(1, 2), (2, 1)]
    swap_x = [(i, i ^ 2) for i in range(8)]
    swap_y = [(i, i ^ 4) for i in range(8)]
    swap_core = [(i, i ^ 1) for i in range(8)]
    forward = [(i, i ^ 2 if i & 1 else i ^ 4) for i in range(8)]

    def gathered(x):
        from_x = lax.ppermute(x, "expert", swap_x)
        from_y = lax.ppermute(x, "expert", swap_y)
        onward = jnp.where(e % 2 == 1, from_y, from_x)
        diagonal = lax.ppermute(onward, "expert", forward)
        near = jnp.concatenate([x, from_x, from_y, diagonal], axis=0)
        return near, lax.ppermute(near, "expert", swap_core)

    finished = [None] * n_quarters
    sent = [None] * n_quarters
    outer = [None] * n_quarters
    inner = [None] * n_quarters
    gains = None
    squares = jnp.zeros((tok, 1), jnp.float32)
    sums = None
    blocks = []
    expert = e.reshape(1).astype(jnp.int32)
    stats = None
    for step in range(n_quarters + 2):
        if step < n_quarters:
            mine = partial(step)
            going = mine.astype(jnp.bfloat16)
            if step == 0:
                gain_row = jnp.concatenate(
                    [norm_gain[None, :], jnp.zeros((15, width), jnp.bfloat16)], axis=0
                )
                going = jnp.concatenate([going, gain_row], axis=0)
            if step >= 2:
                going = jnp.where(is_end, going, sent[step - 2])
            got = lax.ppermute(going, "tensor", both if step >= 2 else inward)
            outer[step] = got
            half_sum = (mine + got[:tok].astype(jnp.float32)).astype(jnp.bfloat16)
            if step == 0:
                outer_gain = got[tok : tok + 1]
                half_sum = jnp.concatenate(
                    [half_sum, norm_gain[None, :], outer_gain, jnp.zeros((14, width), jnp.bfloat16)], axis=0
                )
            inner[step] = lax.ppermute(half_sum, "tensor", middle)
            if step == 0:
                other = inner[0][tok : tok + 1], inner[0][tok + 1 : tok + 2]
                own_gain = norm_gain[None, :]
                gains = (
                    jnp.where(low, outer_gain, other[1]),
                    jnp.where(low, own_gain, other[0]),
                    jnp.where(low, other[0], own_gain),
                    jnp.where(low, other[1], outer_gain),
                )
            hidden = (mine + got[:tok].astype(jnp.float32)) + inner[step][:tok].astype(jnp.float32)
            squares = squares + jnp.sum(hidden * hidden, axis=1, keepdims=True)
            ready = (hidden * gains[step].astype(jnp.float32)).astype(jnp.bfloat16)
            if step == n_quarters - 1:
                high = lax.reduce_precision(squares, 8, 7)
                mid = lax.reduce_precision(squares - high, 8, 7)
                rest = squares - high - mid
                extra = jnp.concatenate(
                    [high, mid, rest, routes.astype(jnp.float32)]
                    + [jnp.full((tok, EXTRA - 3 - routes.shape[1]), -1.0, jnp.float32)],
                    axis=1,
                ).astype(jnp.bfloat16)
                ready = jnp.concatenate([ready, extra], axis=1)
            sent[step] = ready
        else:
            outer_done = lax.ppermute(sent[step - 2], "tensor", outward)
            outer.append(outer_done)
        if step >= 2:
            k = step - 2
            rows = jnp.where(is_end, outer[step], sent[k])
            near, far = gathered(rows)
            blocks.append((near, far))
            last = k == n_quarters - 1
            result = product(near, far, w_gate, w_gate_q, k, width, sums, expert, last)
            if last:
                stats = result
            else:
                sums = result

    ordered = jnp.transpose(stats.reshape(8, 2, 4, tok), (0, 2, 1, 3)).reshape(8, 8, tok)
    routed = stats[2]
    weight = stats[3]
    for bit in range(3):
        flipped = jnp.flip(ordered.reshape(8, 8 >> (bit + 1), 2, 1 << bit, tok), axis=2).reshape(8, 8, tok)
        ordered = jnp.where((e >> bit) & 1 == 1, flipped, ordered)
    expert_sums = jnp.sum(stats[:2] * routed[None, :], axis=1)
    payload = jnp.concatenate(
        [
            ordered[0],
            ordered[1],
            jnp.broadcast_to(expert_sums[None, :], (8, 2)),
            jnp.zeros((8, 126), jnp.float32),
        ],
        axis=1,
    )
    payload = jnp.broadcast_to(payload[:, None, :], (8, 4, 256)).reshape(32, 256)
    back = lax.all_to_all(payload, ("expert", "tensor"), split_axis=0, concat_axis=0, tiled=True)

    def hess_of(k):
        def run():
            near, far = blocks[k]
            half = near.shape[0]
            wide = [part[:, :width].astype(jnp.float32) for part in (near, far)]
            return jnp.sum(wide[0] * wide[0] * weight[:half, None], axis=0) + jnp.sum(
                wide[1] * wide[1] * weight[half:, None], axis=0
            )

        return run

    hess = 2.0 * lax.switch(z, [hess_of(k) for k in range(n_quarters)]) / jnp.sum(routed)
    back = jnp.sum(back.reshape(8, 4, 256), axis=1)
    err, power = back[:, :tok], back[:, tok : 2 * tok]
    ids = jnp.arange(8, dtype=jnp.int32)
    chosen = (routes[:, :, None] == ids[None, None, :]).astype(jnp.float32)
    token_err = jnp.sum(chosen * err.T[:, None, :], axis=2)
    token_pow = jnp.sum(chosen * power.T[:, None, :], axis=2)
    token_error = jnp.sum(route_weights * token_err / (token_pow + epsilon), axis=1)
    own = jnp.sum(jnp.where((ids == e)[:, None], back[:, 2 * tok : 2 * tok + 2], 0.0), axis=0)
    expert_total = own[0] / (own[1] + epsilon)
    return (token_error, expert_total.reshape(1), hess.reshape(1, width))


def solution(mesh):
    placed = (
        P("expert", "tensor"),
        P("tensor", "expert", None),
        P("tensor"),
        P("expert", None),
        P("expert", None),
        P("expert", None, "tensor"),
        P("expert", None, "tensor"),
    )
    on_line = mesh.shape["expert"] == 8 and mesh.shape["tensor"] == 4
    return jax.shard_map(
        line_device if on_line else general_device,
        mesh=mesh,
        in_specs=placed,
        out_specs=(P("expert"), P("expert"), P("expert", "tensor")),
        check_vma=False,
    )
```

```python
import jax
import jax.numpy as jnp
from jax import lax
from jax.experimental import pallas as pl
from jax.experimental.pallas import tpu as pltpu
from jax.sharding import PartitionSpec as P

D = 7168
FF = 2048
CAP = 24
EXTRA = 128


epsilon = 1e-06


def general_device(residual, attn_parts, norm_gain, routes, route_weights, w_gate, w_gate_q):
    n_expert = lax.axis_size("expert")
    tok_count = residual.shape[0]
    local_cols = residual.shape[1]
    top_count = routes.shape[1]
    gain_wide = norm_gain.astype(jnp.float32)[None, :]
    summed = lax.psum_scatter(
        attn_parts[0].astype(jnp.float32).astype(jnp.bfloat16),
        "tensor",
        scatter_dimension=1,
        tiled=True,
    ).astype(jnp.float32)
    hidden = residual.astype(jnp.float32) + summed
    squares = lax.psum(jnp.sum(hidden * hidden, axis=1), "tensor")
    scaling = lax.rsqrt(squares / D + epsilon)
    normed = (hidden * scaling[:, None] * gain_wide).astype(jnp.bfloat16)
    expert_ids = jnp.arange(n_expert, dtype=jnp.int32)
    flat_routes = routes.reshape(-1)
    one_hot = (flat_routes[:, None] == expert_ids[None, :]).astype(jnp.int32)
    earlier = jnp.cumsum(one_hot, axis=0) - one_hot
    slot_index = jnp.sum(earlier * one_hot, axis=1)
    target = flat_routes * CAP + slot_index
    load_counts = jnp.sum(one_hot, axis=0)
    slot_ids = jnp.arange(n_expert * CAP, dtype=jnp.int32)
    placing = (slot_ids[:, None] == target[None, :]).reshape(n_expert * CAP, tok_count, top_count)
    dispatch = jnp.sum(placing.astype(jnp.int32), axis=2).astype(jnp.bfloat16)
    count_send = load_counts.astype(jnp.bfloat16).reshape(n_expert, 1)
    outgoing = jnp.dot(dispatch, normed, preferred_element_type=jnp.float32).astype(jnp.bfloat16)
    outgoing = outgoing.reshape(n_expert, CAP, local_cols)
    arrived, arrived_counts = (
        lax.all_to_all(outgoing, "expert", split_axis=0, concat_axis=0, tiled=True),
        lax.all_to_all(count_send, "expert", split_axis=0, concat_axis=0, tiled=True),
    )
    own_block = arrived.reshape(n_expert * CAP, local_cols)
    column_block = lax.all_gather(own_block, "tensor", axis=1, tiled=True)
    full_acc = jnp.dot(column_block, w_gate[0], preferred_element_type=jnp.float32)
    quant_acc = jnp.dot(column_block, w_gate_q[0], preferred_element_type=jnp.float32)
    block_squares = jnp.einsum("rc,rc->c", own_block, own_block, preferred_element_type=jnp.float32)
    total_load = jnp.sum(arrived_counts.astype(jnp.float32))
    hess_local = 2.0 * block_squares / total_load
    difference = full_acc - quant_acc
    err_part = (jnp.sum(difference * difference, axis=1) / FF).reshape(n_expert, CAP)
    pow_part = (jnp.sum(full_acc * full_acc, axis=1) / FF).reshape(n_expert, CAP)
    err_slots, pow_slots = lax.psum((err_part, pow_part), "tensor")
    expert_total = jnp.sum(err_slots) / (jnp.sum(pow_slots) + epsilon)
    back_err, back_pow = (
        lax.all_to_all(err_slots, "expert", split_axis=0, concat_axis=0, tiled=True),
        lax.all_to_all(pow_slots, "expert", split_axis=0, concat_axis=0, tiled=True),
    )
    token_err = jnp.take(back_err.reshape(-1), target).reshape(tok_count, top_count)
    token_pow = jnp.take(back_pow.reshape(-1), target).reshape(tok_count, top_count)
    ratios = token_err / (token_pow + epsilon)
    token_error = jnp.sum(route_weights * ratios, axis=1)
    return (token_error, expert_total.reshape(1), hess_local.reshape(1, local_cols))


def in_vmem(x):
    return pltpu.with_memory_space_constraint(x, pltpu.VMEM)


def in_hbm(x):
    return pltpu.with_memory_space_constraint(x, pltpu.HBM)


VMEM_SPEC = pl.BlockSpec(memory_space=pltpu.VMEM)
HBM_SPEC = pl.BlockSpec(memory_space=pl.ANY)
SMEM_SPEC = pl.BlockSpec(memory_space=pltpu.SMEM)
TILES = 2


def load_slabs(number_ref, hbm_refs, slab_refs, sems):
    depth, cols = slab_refs[0].shape
    tile = cols // TILES
    start = pl.multiple_of(number_ref[0] * depth, depth)
    copies = []
    for t in range(TILES):
        columns = pl.ds(t * tile, tile)
        for i in range(2):
            copy = pltpu.make_async_copy(
                hbm_refs[i].at[pl.ds(start, depth), columns],
                slab_refs[i].at[:, columns],
                sems.at[2 * t + i],
            )
            copy.start()
            copies.append(copy)
    return copies


def add_kernel(first, depth, number_ref, w_ref, wq_ref, near_ref, far_ref, *refs):
    if first:
        outs, slabs, sems = refs[:2], refs[2:4], refs[4]
    else:
        ins, outs, slabs, sems = refs[:2], refs[2:4], refs[4:6], refs[6]
    copies = load_slabs(number_ref, (w_ref, wq_ref), slabs, sems)
    tile = slabs[0].shape[1] // TILES
    half = near_ref.shape[0]
    for t in range(TILES):
        columns = slice(t * tile, (t + 1) * tile)
        for i in range(2):
            copies[2 * t + i].wait()
            for part, ref in enumerate((near_ref, far_ref)):
                rows = slice(part * half, (part + 1) * half)
                value = jnp.dot(ref[:, :depth], slabs[i][:, columns], preferred_element_type=jnp.float32)
                if not first:
                    value = value + ins[i][rows, columns]
                outs[i][rows, columns] = value


def params():
    return pltpu.CompilerParams(vmem_limit_bytes=24 * 1024 * 1024)


def cost(rows, depth, cols):
    return pl.CostEstimate(flops=4 * rows * depth * cols, bytes_accessed=4 * depth * cols, transcendentals=0)


def add_product(number, w, wq, near, far, sums):
    half, depth = near.shape
    cols = w.shape[1]
    args = [number, in_hbm(w), in_hbm(wq), in_vmem(near), in_vmem(far)]
    args += [in_vmem(x) for x in sums or ()]

    def kernel(*refs):
        add_kernel(not sums, depth, *refs)

    return pl.pallas_call(
        kernel,
        in_specs=[SMEM_SPEC, HBM_SPEC, HBM_SPEC] + [VMEM_SPEC] * (len(args) - 3),
        out_specs=[VMEM_SPEC] * 2,
        out_shape=[pltpu.VMEM((2 * half, cols), jnp.float32)] * 2,
        input_output_aliases={5: 0, 6: 1} if sums else {},
        scratch_shapes=[pltpu.VMEM((depth, cols), w.dtype)] * 2 + [pltpu.SemaphoreType.DMA((2 * TILES,))],
        compiler_params=params(),
        cost_estimate=cost(2 * half, depth, cols),
    )(*args)


def row_stats(depth, expert, rows_ref, slabs, ins, offset, wait):
    half = rows_ref.shape[0]
    tile = slabs[0].shape[1] // TILES
    err = jnp.zeros((half, 1), jnp.float32)
    power = jnp.zeros((half, 1), jnp.float32)
    for t in range(TILES):
        columns = slice(t * tile, (t + 1) * tile)
        made = []
        for i in range(2):
            wait(2 * t + i)
            value = jnp.dot(rows_ref[:, :depth], slabs[i][:, columns], preferred_element_type=jnp.float32)
            made.append(value + ins[i][offset : offset + half, columns])
        diff = made[0] - made[1]
        err = err + jnp.sum(diff * diff, axis=1, keepdims=True)
        power = power + jnp.sum(made[0] * made[0], axis=1, keepdims=True)
    extra = rows_ref[:, depth:].astype(jnp.float32)
    lane = lax.broadcasted_iota(jnp.int32, (half, EXTRA), 1)
    squares = extra[:, 0:1] + extra[:, 1:2] + extra[:, 2:3]
    scale = lax.rsqrt(squares / D + epsilon)
    scale = scale * scale
    named = (lane >= 3) & (extra == expert.astype(jnp.float32))
    routed = jnp.sum(jnp.where(named, 1.0, 0.0), axis=1, keepdims=True)
    stats = jnp.where(lane == 0, err * (scale / FF), 0.0)
    stats = jnp.where(lane == 1, power * (scale / FF), stats)
    stats = jnp.where(lane == 2, routed, stats)
    stats = jnp.where(lane == 3, scale * routed, stats)
    return stats.T[:8, :]


def near_kernel(depth, number_ref, w_ref, wq_ref, near_ref, full_ref, quant_ref, stats_ref, slab, slab_q, sems):
    copies = load_slabs(number_ref, (w_ref, wq_ref), (slab, slab_q), sems)
    stats_ref[...] = row_stats(
        depth, number_ref[1], near_ref, (slab, slab_q), (full_ref, quant_ref), 0, lambda n: copies[n].wait()
    )


def far_kernel(depth, tok, n_z, number_ref, far_ref, full_ref, quant_ref, slab, slab_q, near_stats_ref, stats_ref, out_ref):
    half = far_ref.shape[0]
    expert = number_ref[1]
    far_stats = row_stats(depth, expert, far_ref, (slab, slab_q), (full_ref, quant_ref), half, lambda n: None)
    near_stats = near_stats_ref[...]
    stats_ref[...] = far_stats
    sums = jnp.sum(near_stats * near_stats[2:3, :] + far_stats * far_stats[2:3, :], axis=1, keepdims=True)
    lane = lax.broadcasted_iota(jnp.int32, (8, 2 * tok), 1)
    for part, stats in enumerate((near_stats, far_stats)):
        for pair in range(2):
            both = stats[:, pair * 2 * tok : (pair + 1) * 2 * tok]
            for odd in range(2):
                owner = (4 * pair + 2 * odd + part) ^ expert
                block = jnp.where(lane < tok, pltpu.roll(both, tok, 1) if odd else both, sums)
                for z in range(n_z):
                    out_ref[owner * n_z + z] = block


def finish_kernel(n_z, number_ref, back_ref, routes_ref, weights_ref, token_ref, expert_ref):
    top, tok = routes_ref.shape
    n_expert = back_ref.shape[0] // n_z
    own = jnp.zeros((8, 2 * tok), jnp.float32)
    err = [jnp.zeros((1, tok), jnp.float32)] * top
    power = [jnp.zeros((1, tok), jnp.float32)] * top
    for i in range(n_expert):
        tile = back_ref[i * n_z]
        for z in range(1, n_z):
            tile = tile + back_ref[i * n_z + z]
        own = jnp.where(number_ref[1] == i, tile, own)
        for k in range(top):
            here = routes_ref[k : k + 1, :] == i
            err[k] = jnp.where(here, tile[0:1, :tok], err[k])
            power[k] = jnp.where(here, tile[1:2, :tok], power[k])
    total = jnp.zeros((1, tok), jnp.float32)
    for k in range(top):
        total = total + weights_ref[k : k + 1, :] * (err[k] / (power[k] + epsilon))
    token_ref[...] = total
    expert_ref[...] = own[0:1, tok : tok + 1] / (own[1:2, tok : tok + 1] + epsilon)


def last_product(number, w, wq, near, far_of, sums, n_z):
    half, full_depth = near.shape
    depth = full_depth - EXTRA
    cols = w.shape[1]
    tok = half // 4
    sums = [in_vmem(x) for x in sums]
    slabs = [pltpu.VMEM((depth, cols), w.dtype)] * 2

    def first(*refs):
        near_kernel(depth, *refs)

    near_stats, slab, slab_q = pl.pallas_call(
        first,
        in_specs=[SMEM_SPEC, HBM_SPEC, HBM_SPEC] + [VMEM_SPEC] * 3,
        out_specs=[VMEM_SPEC] * 3,
        out_shape=[pltpu.VMEM((8, half), jnp.float32)] + slabs,
        scratch_shapes=[pltpu.SemaphoreType.DMA((2 * TILES,))],
        compiler_params=params(),
        cost_estimate=cost(half, depth, cols),
    )(number, in_hbm(w), in_hbm(wq), in_vmem(near), *sums)
    far = far_of(near)

    def second(*refs):
        far_kernel(depth, tok, n_z, *refs)

    far_stats, payload = pl.pallas_call(
        second,
        in_specs=[SMEM_SPEC] + [VMEM_SPEC] * 6,
        out_specs=[VMEM_SPEC] * 2,
        out_shape=[
            jax.ShapeDtypeStruct((8, half), jnp.float32),
            jax.ShapeDtypeStruct((8 * n_z, 8, 2 * tok), jnp.float32),
        ],
        compiler_params=params(),
        cost_estimate=cost(half, depth, cols),
    )(number, in_vmem(far), *sums, in_vmem(slab), in_vmem(slab_q), in_vmem(near_stats))
    return near_stats, far_stats, payload


def in_pieces(squares):
    high = lax.reduce_precision(squares, 8, 7)
    mid = lax.reduce_precision(squares - high, 8, 7)
    return [high, mid, squares - high - mid]


def line_device(residual, attn_parts, norm_gain, routes, route_weights, w_gate, w_gate_q):
    z = lax.axis_index("tensor")
    e = lax.axis_index("expert")
    n_z = 4
    tok = residual.shape[0]
    width = residual.shape[1]

    def over_z(x, k):
        return lax.ppermute(x, "tensor", [(i, i ^ k) for i in range(n_z)])

    swap_x = [(i, i ^ 2) for i in range(8)]
    swap_y = [(i, i ^ 4) for i in range(8)]
    swap_core = [(i, i ^ 1) for i in range(8)]
    forward = [(i, i ^ 2 if i & 1 else i ^ 4) for i in range(8)]

    def quarter(k):
        return lax.dynamic_slice(attn_parts[0], (0, (z ^ k) * width), (tok, width))

    arrived = [over_z(quarter(k), k) for k in (3, 2, 1)]
    hidden = residual.astype(jnp.float32) + quarter(0).astype(jnp.float32)
    for part in arrived:
        hidden = hidden + part.astype(jnp.float32)
    squares = jnp.sum(hidden * hidden, axis=1, keepdims=True)
    own = (hidden * norm_gain.astype(jnp.float32)[None, :]).astype(jnp.bfloat16)

    def extra(total):
        return jnp.concatenate(
            in_pieces(total)
            + [routes.astype(jnp.float32)]
            + [jnp.full((tok, EXTRA - 3 - routes.shape[1]), -1.0, jnp.float32)],
            axis=1,
        ).astype(jnp.bfloat16)

    outgoing = jnp.concatenate([own, extra(squares)], axis=1)
    others = [over_z(outgoing, k) for k in (1, 2, 3)]

    def with_total(last):
        total = squares
        for part in (others[0], others[1], last):
            wide = part[:, width : width + 3].astype(jnp.float32)
            total = total + (wide[:, 0:1] + wide[:, 1:2] + wide[:, 2:3])
        return jnp.concatenate([last[:, :width], extra(total)], axis=1)

    blocks = []
    sums = None
    held = None
    for k in range(n_z):
        rows = own if k == 0 else others[k - 1]
        if k:
            rows, _ = lax.optimization_barrier((rows, held))
        if k:
            rows = with_total(rows) if k == n_z - 1 else rows[:, :width]
        if k:
            diagonal = lax.ppermute(held, "expert", forward)
            near = jnp.concatenate(pieces + [diagonal], axis=0)
            if sums:
                near, sums = lax.optimization_barrier((near, sums))
            far = lax.ppermute(near, "expert", swap_core)
            number = jnp.stack([z ^ (k - 1), e]).astype(jnp.int32)
            sums = add_product(number, w_gate[0], w_gate_q[0], near, far, sums)
            blocks.append((near, far))
        from_x = lax.ppermute(rows, "expert", swap_x)
        from_y = lax.ppermute(rows, "expert", swap_y)
        pieces = [rows, from_x, from_y]
        held = jnp.where(e % 2 == 1, from_y, from_x)
    diagonal = lax.ppermute(held, "expert", forward)
    near = jnp.concatenate(pieces + [diagonal], axis=0)
    near, sums = lax.optimization_barrier((near, sums))
    number = jnp.stack([z ^ (n_z - 1), e]).astype(jnp.int32)
    near_stats, far_stats, payload = last_product(
        number, w_gate[0], w_gate_q[0], near, lambda x: lax.ppermute(x, "expert", swap_core), sums, n_z
    )
    back = lax.all_to_all(payload, ("expert", "tensor"), split_axis=0, concat_axis=0, tiled=True)

    hess = 0.0
    for part, stats in zip(blocks[0], (near_stats, far_stats)):
        wide = part.astype(jnp.float32)
        hess = hess + jnp.sum(wide * wide * stats[3][:, None], axis=0)
    hess = 2.0 * hess / (jnp.sum(near_stats[2]) + jnp.sum(far_stats[2]))

    def finish(*refs):
        finish_kernel(n_z, *refs)

    token_error, expert_total = pl.pallas_call(
        finish,
        in_specs=[SMEM_SPEC] + [VMEM_SPEC] * 3,
        out_specs=[VMEM_SPEC] * 2,
        out_shape=[jax.ShapeDtypeStruct((1, tok), jnp.float32), jax.ShapeDtypeStruct((1, 1), jnp.float32)],
    )(number, back, routes.T, route_weights.T)
    return (token_error.reshape(tok), expert_total.reshape(1), hess.reshape(1, width))


def solution(mesh):
    placed = (
        P("expert", "tensor"),
        P("tensor", "expert", None),
        P("tensor"),
        P("expert", None),
        P("expert", None),
        P("expert", None, "tensor"),
        P("expert", None, "tensor"),
    )
    on_line = mesh.shape["expert"] == 8 and mesh.shape["tensor"] == 4
    return jax.shard_map(
        line_device if on_line else general_device,
        mesh=mesh,
        in_specs=placed,
        out_specs=(P("expert"), P("expert"), P("expert", "tensor")),
        check_vma=False,
    )
```

```python
import jax
import jax.numpy as jnp
from jax import lax
from jax.experimental import pallas as pl
from jax.experimental.pallas import tpu as pltpu
from jax.sharding import PartitionSpec as P

D = 7168
FF = 2048
CAP = 24
EXTRA = 128


epsilon = 1e-06


def general_device(residual, attn_parts, norm_gain, routes, route_weights, w_gate, w_gate_q):
    n_expert = lax.axis_size("expert")
    tok_count = residual.shape[0]
    local_cols = residual.shape[1]
    top_count = routes.shape[1]
    gain_wide = norm_gain.astype(jnp.float32)[None, :]
    summed = lax.psum_scatter(
        attn_parts[0].astype(jnp.float32).astype(jnp.bfloat16),
        "tensor",
        scatter_dimension=1,
        tiled=True,
    ).astype(jnp.float32)
    hidden = residual.astype(jnp.float32) + summed
    squares = lax.psum(jnp.sum(hidden * hidden, axis=1), "tensor")
    scaling = lax.rsqrt(squares / D + epsilon)
    normed = (hidden * scaling[:, None] * gain_wide).astype(jnp.bfloat16)
    expert_ids = jnp.arange(n_expert, dtype=jnp.int32)
    flat_routes = routes.reshape(-1)
    one_hot = (flat_routes[:, None] == expert_ids[None, :]).astype(jnp.int32)
    earlier = jnp.cumsum(one_hot, axis=0) - one_hot
    slot_index = jnp.sum(earlier * one_hot, axis=1)
    target = flat_routes * CAP + slot_index
    load_counts = jnp.sum(one_hot, axis=0)
    slot_ids = jnp.arange(n_expert * CAP, dtype=jnp.int32)
    placing = (slot_ids[:, None] == target[None, :]).reshape(n_expert * CAP, tok_count, top_count)
    dispatch = jnp.sum(placing.astype(jnp.int32), axis=2).astype(jnp.bfloat16)
    count_send = load_counts.astype(jnp.bfloat16).reshape(n_expert, 1)
    outgoing = jnp.dot(dispatch, normed, preferred_element_type=jnp.float32).astype(jnp.bfloat16)
    outgoing = outgoing.reshape(n_expert, CAP, local_cols)
    arrived, arrived_counts = (
        lax.all_to_all(outgoing, "expert", split_axis=0, concat_axis=0, tiled=True),
        lax.all_to_all(count_send, "expert", split_axis=0, concat_axis=0, tiled=True),
    )
    own_block = arrived.reshape(n_expert * CAP, local_cols)
    column_block = lax.all_gather(own_block, "tensor", axis=1, tiled=True)
    full_acc = jnp.dot(column_block, w_gate[0], preferred_element_type=jnp.float32)
    quant_acc = jnp.dot(column_block, w_gate_q[0], preferred_element_type=jnp.float32)
    block_squares = jnp.einsum("rc,rc->c", own_block, own_block, preferred_element_type=jnp.float32)
    total_load = jnp.sum(arrived_counts.astype(jnp.float32))
    hess_local = 2.0 * block_squares / total_load
    difference = full_acc - quant_acc
    err_part = (jnp.sum(difference * difference, axis=1) / FF).reshape(n_expert, CAP)
    pow_part = (jnp.sum(full_acc * full_acc, axis=1) / FF).reshape(n_expert, CAP)
    err_slots, pow_slots = lax.psum((err_part, pow_part), "tensor")
    expert_total = jnp.sum(err_slots) / (jnp.sum(pow_slots) + epsilon)
    back_err, back_pow = (
        lax.all_to_all(err_slots, "expert", split_axis=0, concat_axis=0, tiled=True),
        lax.all_to_all(pow_slots, "expert", split_axis=0, concat_axis=0, tiled=True),
    )
    token_err = jnp.take(back_err.reshape(-1), target).reshape(tok_count, top_count)
    token_pow = jnp.take(back_pow.reshape(-1), target).reshape(tok_count, top_count)
    ratios = token_err / (token_pow + epsilon)
    token_error = jnp.sum(route_weights * ratios, axis=1)
    return (token_error, expert_total.reshape(1), hess_local.reshape(1, local_cols))


def in_vmem(x):
    return pltpu.with_memory_space_constraint(x, pltpu.VMEM)


def in_hbm(x):
    return pltpu.with_memory_space_constraint(x, pltpu.HBM)


VMEM_SPEC = pl.BlockSpec(memory_space=pltpu.VMEM)
HBM_SPEC = pl.BlockSpec(memory_space=pl.ANY)
SMEM_SPEC = pl.BlockSpec(memory_space=pltpu.SMEM)
PARAMS = pltpu.CompilerParams(vmem_limit_bytes=24 * 1024 * 1024)


def cost(rows, depth, cols):
    return pl.CostEstimate(flops=4 * rows * depth * cols, bytes_accessed=4 * depth * cols, transcendentals=0)


def start_slab(number, hbm_ref, slab_ref, sem):
    depth = slab_ref.shape[0]
    first = pl.multiple_of(number * depth, depth)
    copy = pltpu.make_async_copy(hbm_ref.at[pl.ds(first, depth), :], slab_ref, sem)
    copy.start()
    return copy


def load_kernel(numbers_ref, w_ref, wq_ref, slab_ref, slab_q_ref, sems):
    copies = [
        start_slab(numbers_ref[1], w_ref, slab_ref, sems.at[0]),
        start_slab(numbers_ref[1], wq_ref, slab_q_ref, sems.at[1]),
    ]
    for copy in copies:
        copy.wait()


def load_product(numbers, w, wq, depth):
    return pl.pallas_call(
        load_kernel,
        in_specs=[SMEM_SPEC, HBM_SPEC, HBM_SPEC],
        out_specs=[VMEM_SPEC] * 2,
        out_shape=[pltpu.VMEM((depth, w.shape[1]), w.dtype)] * 2,
        scratch_shapes=[pltpu.SemaphoreType.DMA((2,))],
        compiler_params=PARAMS,
        cost_estimate=cost(0, depth, w.shape[1]),
    )(numbers, in_hbm(w), in_hbm(wq))


def first_product(rows, slabs):
    count = rows.shape[0]
    depth, cols = slabs[0].shape

    def kernel(rows_ref, slab_ref, slab_q_ref, full_ref, quant_ref, tail_ref):
        half = count // 2
        for part in range(2):
            here = slice(part * half, (part + 1) * half)
            x = rows_ref[here, :depth]
            full_ref[here, :] = jnp.dot(x, slab_ref[...], preferred_element_type=jnp.float32)
            quant_ref[here, :] = jnp.dot(x, slab_q_ref[...], preferred_element_type=jnp.float32)
        tail_ref[...] = rows_ref[:, depth:].astype(jnp.float32)

    return pl.pallas_call(
        kernel,
        in_specs=[VMEM_SPEC] * 3,
        out_specs=[VMEM_SPEC] * 3,
        out_shape=[pltpu.VMEM((count, cols), jnp.float32)] * 2 + [pltpu.VMEM((count, EXTRA), jnp.float32)],
        compiler_params=PARAMS,
        cost_estimate=cost(count, depth, cols),
    )(*[in_vmem(x) for x in (rows, *slabs)])


def fetching(numbers_ref, hbm_refs, slabs, sems, first):
    copies = []
    for n, slab in enumerate(slabs):
        copies.append(start_slab(numbers_ref[first + n // 2], hbm_refs[n % 2], slab, sems.at[n]))
    return copies


def add_product(numbers, w, wq, rows, depth, sums):
    count = rows[0].shape[0]
    cols = w.shape[1]
    quarters = len(rows)

    def kernel(numbers_ref, w_ref, wq_ref, *refs):
        row_refs, ins, outs = refs[:quarters], refs[quarters : quarters + 3], refs[quarters + 3 : quarters + 6]
        slabs, sems = refs[quarters + 6 : -1], refs[-1]
        copies = fetching(numbers_ref, (w_ref, wq_ref), slabs, sems, 2)
        half = count // 2
        for q in range(quarters):
            for i in range(2):
                copies[2 * q + i].wait()
                before = outs[i] if q else ins[i]
                for part in range(2):
                    here = slice(part * half, (part + 1) * half)
                    outs[i][here, :] = before[here, :] + jnp.dot(
                        row_refs[q][here, :depth], slabs[2 * q + i][...], preferred_element_type=jnp.float32
                    )
        tail = ins[2][:count, :]
        for ref in row_refs:
            tail = tail + ref[:, depth:].astype(jnp.float32)
        outs[2][...] = tail

    return pl.pallas_call(
        kernel,
        in_specs=[SMEM_SPEC, HBM_SPEC, HBM_SPEC] + [VMEM_SPEC] * (quarters + 3),
        out_specs=[VMEM_SPEC] * 3,
        out_shape=[pltpu.VMEM((count, cols), jnp.float32)] * 2 + [pltpu.VMEM((count, EXTRA), jnp.float32)],
        scratch_shapes=[pltpu.VMEM((depth, cols), w.dtype)] * (2 * quarters)
        + [pltpu.SemaphoreType.DMA((2 * quarters,))],
        compiler_params=PARAMS,
        cost_estimate=cost(count * quarters, depth, cols),
    )(numbers, in_hbm(w), in_hbm(wq), *[in_vmem(x) for x in (*rows, *sums)])


def row_stats(expert, full, quant, total, extra):
    count = full.shape[0]
    diff = full - quant
    err = jnp.sum(diff * diff, axis=1, keepdims=True)
    power = jnp.sum(full * full, axis=1, keepdims=True)
    lane = lax.broadcasted_iota(jnp.int32, (count, EXTRA), 1)
    squares = total[:, 0:1] + total[:, 1:2] + total[:, 2:3]
    scale = lax.rsqrt(squares / D + epsilon)
    scale = scale * scale
    named = (lane >= 3) & (extra == expert.astype(jnp.float32))
    routed = jnp.sum(jnp.where(named, 1.0, 0.0), axis=1, keepdims=True)
    stats = jnp.where(lane == 0, err * (scale / FF), 0.0)
    stats = jnp.where(lane == 1, power * (scale / FF), stats)
    stats = jnp.where(lane == 2, routed, stats)
    stats = jnp.where(lane == 3, scale * routed, stats)
    return stats.T[:8, :]


def early_stats(numbers, w, wq, rows, depth, sums, n_z):
    count = rows.shape[0]
    cols = w.shape[1]
    kept = 2 * (n_z - 1)

    def kernel(numbers_ref, w_ref, wq_ref, rows_ref, full_ref, quant_ref, tail_ref, stats_ref, *refs):
        slabs, sems = refs[:kept], refs[kept]
        last = fetching(numbers_ref, (w_ref, wq_ref), slabs[kept - 2 :], sems.at[pl.ds(kept - 2, 2)], n_z)
        others = fetching(numbers_ref, (w_ref, wq_ref), slabs[: kept - 2], sems, 2)
        x = rows_ref[:, :depth]
        made = []
        for i, before in enumerate((full_ref, quant_ref)):
            last[i].wait()
            made.append(before[...] + jnp.dot(x, slabs[kept - 2 + i][...], preferred_element_type=jnp.float32))
        extra = rows_ref[:, depth:].astype(jnp.float32)
        stats_ref[...] = row_stats(numbers_ref[0], *made, tail_ref[...] + extra, extra)
        for copy in others:
            copy.wait()

    out = pl.pallas_call(
        kernel,
        in_specs=[SMEM_SPEC, HBM_SPEC, HBM_SPEC] + [VMEM_SPEC] * 4,
        out_specs=[VMEM_SPEC] * (1 + kept),
        out_shape=[pltpu.VMEM((8, count), jnp.float32)] + [pltpu.VMEM((depth, cols), w.dtype)] * kept,
        scratch_shapes=[pltpu.SemaphoreType.DMA((kept,))],
        compiler_params=PARAMS,
        cost_estimate=cost(count, depth, cols),
    )(numbers, in_hbm(w), in_hbm(wq), *[in_vmem(x) for x in (rows, *sums)])
    return out[0], out[1:]


def late_stats(numbers, rows, slabs, sums, early, tok, n_z):
    quarters = len(rows)
    count = rows[0].shape[0]
    depth, cols = slabs[0].shape

    def kernel(numbers_ref, *refs):
        row_refs, slab_refs = refs[:quarters], refs[quarters : 3 * quarters]
        full_ref, quant_ref, tail_ref, early_ref, stats_ref, out_ref = refs[3 * quarters :]
        expert = numbers_ref[0]
        core = expert % 2
        before = early_ref[...]
        here = slice(before.shape[1], before.shape[1] + count)
        total = tail_ref[here, :]
        made = [full_ref[here, :], quant_ref[here, :]]
        for q, ref in enumerate(row_refs):
            extra = ref[:, depth:].astype(jnp.float32)
            total = total + extra
            for i in range(2):
                made[i] = made[i] + jnp.dot(
                    ref[:, :depth], slab_refs[2 * q + i][...], preferred_element_type=jnp.float32
                )
        stats = row_stats(expert, *made, total, extra)
        stats_ref[...] = stats
        sums_early = jnp.sum(before * before[2:3, :], axis=1, keepdims=True)
        sums_here = sums_early + jnp.sum(stats * stats[2:3, :], axis=1, keepdims=True)
        lane = lax.broadcasted_iota(jnp.int32, (8, 2 * tok), 1)
        order = ((0, 0), (1, 1), (2, 4), (3, 5), (5, 3), (4, 2), (6, 6), (7, 7))
        for pair in range(4):
            both = stats if pair == 3 else before[:, pair * 2 * tok : (pair + 1) * 2 * tok]
            for odd in range(2):
                zero, one = order[2 * pair + odd]
                owner = expert ^ (zero + core * (one - zero))
                block = jnp.where(lane < tok, pltpu.roll(both, tok, 1) if odd else both, sums_here)
                for z in range(n_z):
                    out_ref[owner * n_z + z] = block

    return pl.pallas_call(
        kernel,
        in_specs=[SMEM_SPEC] + [VMEM_SPEC] * (3 * quarters + 4),
        out_specs=[VMEM_SPEC] * 2,
        out_shape=[
            pltpu.VMEM((8, count), jnp.float32),
            jax.ShapeDtypeStruct((8 * n_z, 8, 2 * tok), jnp.float32),
        ],
        compiler_params=PARAMS,
        cost_estimate=cost(count, depth, cols),
    )(numbers, *[in_vmem(x) for x in (*rows, *slabs, *sums, early)])


def hessian(rows, early, late, width):
    def kernel(rows_ref, early_ref, late_ref, out_ref):
        split = early_ref.shape[1]
        total = jnp.sum(early_ref[2:3, :], axis=1, keepdims=True) + jnp.sum(
            late_ref[2:3, :], axis=1, keepdims=True
        )
        weight_early = early_ref[...].T[:, 3:4]
        weight_late = late_ref[...].T[:, 3:4]
        step = 256
        for first in range(0, width, step):
            columns = slice(first, first + step)
            x = rows_ref[:split, columns].astype(jnp.float32)
            y = rows_ref[split:, columns].astype(jnp.float32)
            value = jnp.sum(x * x * weight_early, axis=0, keepdims=True)
            value = value + jnp.sum(y * y * weight_late, axis=0, keepdims=True)
            out_ref[:, columns] = 2.0 * value / total

    return pl.pallas_call(
        kernel,
        in_specs=[VMEM_SPEC] * 3,
        out_specs=VMEM_SPEC,
        out_shape=jax.ShapeDtypeStruct((1, width), jnp.float32),
        compiler_params=PARAMS,
        cost_estimate=pl.CostEstimate(flops=4 * rows.size, bytes_accessed=2 * rows.size, transcendentals=0),
    )(rows, in_vmem(early), in_vmem(late))


def finish(numbers, back, routes, weights, n_z):
    top, tok = routes.shape

    def kernel(numbers_ref, back_ref, routes_ref, weights_ref, token_ref, expert_ref):
        own = jnp.zeros((8, 2 * tok), jnp.float32)
        err = [jnp.zeros((1, tok), jnp.float32)] * top
        power = [jnp.zeros((1, tok), jnp.float32)] * top
        for i in range(back_ref.shape[0] // n_z):
            tile = back_ref[i * n_z]
            for z in range(1, n_z):
                tile = tile + back_ref[i * n_z + z]
            own = jnp.where(numbers_ref[0] == i, tile, own)
            for k in range(top):
                here = routes_ref[k : k + 1, :] == i
                err[k] = jnp.where(here, tile[0:1, :tok], err[k])
                power[k] = jnp.where(here, tile[1:2, :tok], power[k])
        total = jnp.zeros((1, tok), jnp.float32)
        for k in range(top):
            total = total + weights_ref[k : k + 1, :] * (err[k] / (power[k] + epsilon))
        token_ref[...] = total
        expert_ref[...] = own[0:1, tok : tok + 1] / (own[1:2, tok : tok + 1] + epsilon)

    return pl.pallas_call(
        kernel,
        in_specs=[SMEM_SPEC] + [VMEM_SPEC] * 3,
        out_specs=[VMEM_SPEC] * 2,
        out_shape=[jax.ShapeDtypeStruct((1, tok), jnp.float32), jax.ShapeDtypeStruct((1, 1), jnp.float32)],
    )(numbers, back, in_vmem(routes), in_vmem(weights))


def in_pieces(squares):
    high = lax.reduce_precision(squares, 8, 7)
    mid = lax.reduce_precision(squares - high, 8, 7)
    return [high, mid, squares - high - mid]


def line_device(residual, attn_parts, norm_gain, routes, route_weights, w_gate, w_gate_q):
    z = lax.axis_index("tensor")
    e = lax.axis_index("expert")
    n_z = 4
    tok = residual.shape[0]
    width = residual.shape[1]

    def over_z(x, k):
        return lax.ppermute(x, "tensor", [(i, i ^ k) for i in range(n_z)])

    def in_plane(x, zero, one):
        return lax.ppermute(x, "expert", [(i, i ^ (one if i & 1 else zero)) for i in range(8)])

    def quarter(k):
        return lax.dynamic_slice(attn_parts[0], (0, (z ^ k) * width), (tok, width))

    numbers = jnp.stack([e, z, z ^ 1, z ^ 2, z ^ 3]).astype(jnp.int32)
    w, wq = w_gate[0], w_gate_q[0]

    arrived = [over_z(quarter(k), k) for k in (3, 2, 1)]
    slabs = load_product(numbers, w, wq, width)
    residual, *slabs = lax.optimization_barrier((residual, *slabs))
    hidden = residual.astype(jnp.float32) + quarter(0).astype(jnp.float32)
    for part in arrived:
        hidden = hidden + part.astype(jnp.float32)
    squares = jnp.sum(hidden * hidden, axis=1, keepdims=True)
    own = (hidden * norm_gain.astype(jnp.float32)[None, :]).astype(jnp.bfloat16)
    extra = jnp.concatenate(
        in_pieces(squares)
        + [routes.astype(jnp.float32)]
        + [jnp.full((tok, EXTRA - 3 - routes.shape[1]), -1.0, jnp.float32)],
        axis=1,
    ).astype(jnp.bfloat16)
    own = jnp.concatenate([own, extra], axis=1)
    z_near, z_far = over_z(own, 1), over_z(own, 2)
    z_both = over_z(z_far, 1)

    def other_core(rows):
        return in_plane(rows, 1, 1)

    def next_chip(rows):
        return in_plane(rows, 2, 4)

    def opposite(rows):
        return in_plane(rows, 4, 2)

    def tied(x, *values):
        return lax.optimization_barrier((x, *values))[0]

    def most(near, beside):
        return (*near, *beside, *map(other_core, beside))

    near = own, other_core(own)
    beside = next_chip(near[0]), next_chip(near[1])
    across = opposite(beside[0])
    rows = jnp.concatenate([*most(near, beside), across, other_core(across)], axis=0)
    first_sums = first_product(rows, slabs)

    def of_quarters(parts):
        return [jnp.concatenate([x[q * tok : (q + 1) * tok] for x in parts], axis=0) for q in range(2)]

    pair = tied(jnp.concatenate([z_near, z_far], axis=0), *beside)
    near = pair, other_core(pair)
    beside = next_chip(near[0]), next_chip(near[1])
    across = opposite(tied(*beside, *first_sums))
    gathered = most(near, beside)
    sums = add_product(numbers, w, wq, of_quarters(gathered), width, first_sums)
    last = of_quarters((across, other_core(across)))

    single = tied(z_both, beside[1])
    near = single, tied(other_core(single), gathered[4], gathered[5])
    beside = next_chip(near[0]), next_chip(near[1])
    across = opposite(tied(*beside, *sums))
    early, slabs = early_stats(numbers, w, wq, jnp.concatenate(most(near, beside), axis=0), width, sums, n_z)
    last.append(jnp.concatenate([across, other_core(tied(across, early))], axis=0))
    late, payload = late_stats(numbers, last, slabs, first_sums, early, tok, n_z)

    back = lax.all_to_all(payload, ("expert", "tensor"), split_axis=0, concat_axis=0, tiled=True)
    hess = hessian(rows, early, late, width)
    token_error, expert_total = finish(numbers, back, routes.T, route_weights.T, n_z)
    return (token_error.reshape(tok), expert_total.reshape(1), hess.reshape(1, width))


def solution(mesh):
    placed = (
        P("expert", "tensor"),
        P("tensor", "expert", None),
        P("tensor"),
        P("expert", None),
        P("expert", None),
        P("expert", None, "tensor"),
        P("expert", None, "tensor"),
    )
    on_line = mesh.shape["expert"] == 8 and mesh.shape["tensor"] == 4
    return jax.shard_map(
        line_device if on_line else general_device,
        mesh=mesh,
        in_specs=placed,
        out_specs=(P("expert"), P("expert"), P("expert", "tensor")),
        check_vma=False,
    )
```

```python
import jax
import jax.numpy as jnp
from jax import lax
from jax.experimental import pallas as pl
from jax.experimental.pallas import tpu as pltpu
from jax.sharding import PartitionSpec as P

D = 7168
FF = 2048
CAP = 24
EXTRA = 128


epsilon = 1e-06


def general_device(residual, attn_parts, norm_gain, routes, route_weights, w_gate, w_gate_q):
    n_expert = lax.axis_size("expert")
    tok_count = residual.shape[0]
    local_cols = residual.shape[1]
    top_count = routes.shape[1]
    gain_wide = norm_gain.astype(jnp.float32)[None, :]
    summed = lax.psum_scatter(
        attn_parts[0].astype(jnp.float32).astype(jnp.bfloat16),
        "tensor",
        scatter_dimension=1,
        tiled=True,
    ).astype(jnp.float32)
    hidden = residual.astype(jnp.float32) + summed
    squares = lax.psum(jnp.sum(hidden * hidden, axis=1), "tensor")
    scaling = lax.rsqrt(squares / D + epsilon)
    normed = (hidden * scaling[:, None] * gain_wide).astype(jnp.bfloat16)
    expert_ids = jnp.arange(n_expert, dtype=jnp.int32)
    flat_routes = routes.reshape(-1)
    one_hot = (flat_routes[:, None] == expert_ids[None, :]).astype(jnp.int32)
    earlier = jnp.cumsum(one_hot, axis=0) - one_hot
    slot_index = jnp.sum(earlier * one_hot, axis=1)
    target = flat_routes * CAP + slot_index
    load_counts = jnp.sum(one_hot, axis=0)
    slot_ids = jnp.arange(n_expert * CAP, dtype=jnp.int32)
    placing = (slot_ids[:, None] == target[None, :]).reshape(n_expert * CAP, tok_count, top_count)
    dispatch = jnp.sum(placing.astype(jnp.int32), axis=2).astype(jnp.bfloat16)
    count_send = load_counts.astype(jnp.bfloat16).reshape(n_expert, 1)
    outgoing = jnp.dot(dispatch, normed, preferred_element_type=jnp.float32).astype(jnp.bfloat16)
    outgoing = outgoing.reshape(n_expert, CAP, local_cols)
    arrived, arrived_counts = (
        lax.all_to_all(outgoing, "expert", split_axis=0, concat_axis=0, tiled=True),
        lax.all_to_all(count_send, "expert", split_axis=0, concat_axis=0, tiled=True),
    )
    own_block = arrived.reshape(n_expert * CAP, local_cols)
    column_block = lax.all_gather(own_block, "tensor", axis=1, tiled=True)
    full_acc = jnp.dot(column_block, w_gate[0], preferred_element_type=jnp.float32)
    quant_acc = jnp.dot(column_block, w_gate_q[0], preferred_element_type=jnp.float32)
    block_squares = jnp.einsum("rc,rc->c", own_block, own_block, preferred_element_type=jnp.float32)
    total_load = jnp.sum(arrived_counts.astype(jnp.float32))
    hess_local = 2.0 * block_squares / total_load
    difference = full_acc - quant_acc
    err_part = (jnp.sum(difference * difference, axis=1) / FF).reshape(n_expert, CAP)
    pow_part = (jnp.sum(full_acc * full_acc, axis=1) / FF).reshape(n_expert, CAP)
    err_slots, pow_slots = lax.psum((err_part, pow_part), "tensor")
    expert_total = jnp.sum(err_slots) / (jnp.sum(pow_slots) + epsilon)
    back_err, back_pow = (
        lax.all_to_all(err_slots, "expert", split_axis=0, concat_axis=0, tiled=True),
        lax.all_to_all(pow_slots, "expert", split_axis=0, concat_axis=0, tiled=True),
    )
    token_err = jnp.take(back_err.reshape(-1), target).reshape(tok_count, top_count)
    token_pow = jnp.take(back_pow.reshape(-1), target).reshape(tok_count, top_count)
    ratios = token_err / (token_pow + epsilon)
    token_error = jnp.sum(route_weights * ratios, axis=1)
    return (token_error, expert_total.reshape(1), hess_local.reshape(1, local_cols))


def in_vmem(x):
    return pltpu.with_memory_space_constraint(x, pltpu.VMEM)


def in_hbm(x):
    return pltpu.with_memory_space_constraint(x, pltpu.HBM)


VMEM_SPEC = pl.BlockSpec(memory_space=pltpu.VMEM)
HBM_SPEC = pl.BlockSpec(memory_space=pl.ANY)
SMEM_SPEC = pl.BlockSpec(memory_space=pltpu.SMEM)
PARAMS = pltpu.CompilerParams(vmem_limit_bytes=24 * 1024 * 1024)


def cost(rows, depth, cols):
    return pl.CostEstimate(flops=4 * rows * depth * cols, bytes_accessed=4 * depth * cols, transcendentals=0)


def start_slab(number, hbm_ref, slab_ref, sem):
    depth = slab_ref.shape[0]
    first = pl.multiple_of(number * depth, depth)
    copy = pltpu.make_async_copy(hbm_ref.at[pl.ds(first, depth), :], slab_ref, sem)
    copy.start()
    return copy


def load_kernel(numbers_ref, w_ref, wq_ref, slab_ref, slab_q_ref, sems):
    copies = [
        start_slab(numbers_ref[1], w_ref, slab_ref, sems.at[0]),
        start_slab(numbers_ref[1], wq_ref, slab_q_ref, sems.at[1]),
    ]
    for copy in copies:
        copy.wait()


def load_product(numbers, w, wq, depth):
    return pl.pallas_call(
        load_kernel,
        in_specs=[SMEM_SPEC, HBM_SPEC, HBM_SPEC],
        out_specs=[VMEM_SPEC] * 2,
        out_shape=[pltpu.VMEM((depth, w.shape[1]), w.dtype)] * 2,
        scratch_shapes=[pltpu.SemaphoreType.DMA((2,))],
        compiler_params=PARAMS,
        cost_estimate=cost(0, depth, w.shape[1]),
    )(numbers, in_hbm(w), in_hbm(wq))


def first_product(rows, slabs):
    count = rows.shape[0]
    depth, cols = slabs[0].shape

    def kernel(rows_ref, slab_ref, slab_q_ref, full_ref, quant_ref, tail_ref):
        half = count // 2
        for part in range(2):
            here = slice(part * half, (part + 1) * half)
            x = rows_ref[here, :depth]
            full_ref[here, :] = jnp.dot(x, slab_ref[...], preferred_element_type=jnp.float32)
            quant_ref[here, :] = jnp.dot(x, slab_q_ref[...], preferred_element_type=jnp.float32)
        tail_ref[...] = rows_ref[:, depth:].astype(jnp.float32)

    return pl.pallas_call(
        kernel,
        in_specs=[VMEM_SPEC] * 3,
        out_specs=[VMEM_SPEC] * 3,
        out_shape=[pltpu.VMEM((count, cols), jnp.float32)] * 2 + [pltpu.VMEM((count, EXTRA), jnp.float32)],
        compiler_params=PARAMS,
        cost_estimate=cost(count, depth, cols),
    )(*[in_vmem(x) for x in (rows, *slabs)])


def fetching(numbers_ref, hbm_refs, slabs, sems, first):
    copies = []
    for n, slab in enumerate(slabs):
        copies.append(start_slab(numbers_ref[first + n // 2], hbm_refs[n % 2], slab, sems.at[n]))
    return copies


def add_product(numbers, w, wq, rows, depth, sums):
    count = rows[0].shape[0]
    cols = w.shape[1]
    quarters = len(rows)
    kept = 2 * quarters + 2

    def kernel(numbers_ref, w_ref, wq_ref, *refs):
        row_refs, ins, outs = refs[:quarters], refs[quarters : quarters + 3], refs[quarters + 3 : quarters + 6]
        slabs, sems = refs[quarters + 6 : -1], refs[-1]
        copies = fetching(numbers_ref, (w_ref, wq_ref), slabs, sems, 2)
        for q in range(quarters):
            for i in range(2):
                copies[2 * q + i].wait()
                before = outs[i][...] if q else ins[i][:count, :]
                outs[i][...] = before + jnp.dot(
                    row_refs[q][:, :depth], slabs[2 * q + i][...], preferred_element_type=jnp.float32
                )
        tail = ins[2][:count, :]
        for ref in row_refs:
            tail = tail + ref[:, depth:].astype(jnp.float32)
        outs[2][...] = tail
        for copy in copies[2 * quarters :]:
            copy.wait()

    out = pl.pallas_call(
        kernel,
        in_specs=[SMEM_SPEC, HBM_SPEC, HBM_SPEC] + [VMEM_SPEC] * (quarters + 3),
        out_specs=[VMEM_SPEC] * (3 + kept),
        out_shape=[pltpu.VMEM((count, cols), jnp.float32)] * 2
        + [pltpu.VMEM((count, EXTRA), jnp.float32)]
        + [pltpu.VMEM((depth, cols), w.dtype)] * kept,
        scratch_shapes=[pltpu.SemaphoreType.DMA((kept,))],
        compiler_params=PARAMS,
        cost_estimate=cost(count * quarters, depth, cols),
    )(numbers, in_hbm(w), in_hbm(wq), *[in_vmem(x) for x in (*rows, *sums)])
    return out[3:], out[:3]


def row_stats(expert, full, quant, total, extra):
    count = full.shape[0]
    diff = full - quant
    err = jnp.sum(diff * diff, axis=1, keepdims=True)
    power = jnp.sum(full * full, axis=1, keepdims=True)
    lane = lax.broadcasted_iota(jnp.int32, (count, EXTRA), 1)
    squares = total[:, 0:1] + total[:, 1:2] + total[:, 2:3]
    scale = lax.rsqrt(squares / D + epsilon)
    scale = scale * scale
    named = (lane >= 3) & (extra == expert.astype(jnp.float32))
    routed = jnp.sum(jnp.where(named, 1.0, 0.0), axis=1, keepdims=True)
    stats = jnp.where(lane == 0, err * (scale / FF), 0.0)
    stats = jnp.where(lane == 1, power * (scale / FF), stats)
    stats = jnp.where(lane == 2, routed, stats)
    stats = jnp.where(lane == 3, scale * routed, stats)
    return stats.T[:8, :]


def early_stats(numbers, rows, rest, slabs, sums, first_sums):
    count = rows.shape[0]
    done = sums[0].shape[0]
    depth, cols = slabs[0].shape
    quarters = len(rest)

    def kernel(numbers_ref, rows_ref, *refs):
        rest_refs, refs = refs[:quarters], refs[quarters:]
        slab_refs, ins, firsts, stats_ref = refs[: len(slabs)], refs[-7:-4], refs[-4:-1], refs[-1]
        expert = numbers_ref[0]
        here = slice(0, done)
        made = [
            before[...] + jnp.dot(rows_ref[here, :depth], slab[...], preferred_element_type=jnp.float32)
            for before, slab in zip(ins[:2], slab_refs[-2:])
        ]
        extra = rows_ref[here, depth:].astype(jnp.float32)
        stats_ref[:, here] = row_stats(expert, *made, ins[2][...] + extra, extra)
        here = slice(done, count)
        made = [
            before[here, :] + jnp.dot(rows_ref[here, :depth], slab[...], preferred_element_type=jnp.float32)
            for before, slab in zip(firsts[:2], slab_refs[-2:])
        ]
        extra = rows_ref[here, depth:].astype(jnp.float32)
        total = firsts[2][here, :] + extra
        for q, ref in enumerate(rest_refs):
            total = total + ref[:, depth:].astype(jnp.float32)
            for i in range(2):
                made[i] = made[i] + jnp.dot(
                    ref[:, :depth], slab_refs[2 * q + i][...], preferred_element_type=jnp.float32
                )
        stats_ref[:, here] = row_stats(expert, *made, total, extra)

    args = [rows, *rest, *slabs, *sums, *first_sums]
    return pl.pallas_call(
        kernel,
        in_specs=[SMEM_SPEC] + [VMEM_SPEC] * len(args),
        out_specs=VMEM_SPEC,
        out_shape=pltpu.VMEM((8, count), jnp.float32),
        compiler_params=PARAMS,
        cost_estimate=cost(count, depth, cols),
    )(numbers, *[in_vmem(x) for x in args])


def late_stats(numbers, rows, slabs, sums, early, tok, n_z):
    quarters = len(rows)
    count = rows[0].shape[0]
    depth, cols = slabs[0].shape

    def kernel(numbers_ref, *refs):
        row_refs, slab_refs = refs[:quarters], refs[quarters : 3 * quarters]
        full_ref, quant_ref, tail_ref, early_ref, stats_ref, out_ref = refs[3 * quarters :]
        expert = numbers_ref[0]
        core = expert % 2
        before = early_ref[...]
        here = slice(before.shape[1], before.shape[1] + count)
        total = tail_ref[here, :]
        made = [full_ref[here, :], quant_ref[here, :]]
        for q, ref in enumerate(row_refs):
            extra = ref[:, depth:].astype(jnp.float32)
            total = total + extra
            for i in range(2):
                made[i] = made[i] + jnp.dot(
                    ref[:, :depth], slab_refs[2 * q + i][...], preferred_element_type=jnp.float32
                )
        stats = row_stats(expert, *made, total, extra)
        stats_ref[...] = stats
        sums_early = jnp.sum(before * before[2:3, :], axis=1, keepdims=True)
        sums_here = sums_early + jnp.sum(stats * stats[2:3, :], axis=1, keepdims=True)
        lane = lax.broadcasted_iota(jnp.int32, (8, 2 * tok), 1)
        order = ((0, 0), (1, 1), (2, 4), (3, 5), (5, 3), (4, 2), (6, 6), (7, 7))
        for pair in range(4):
            both = stats if pair == 3 else before[:, pair * 2 * tok : (pair + 1) * 2 * tok]
            for odd in range(2):
                zero, one = order[2 * pair + odd]
                owner = expert ^ (zero + core * (one - zero))
                block = jnp.where(lane < tok, pltpu.roll(both, tok, 1) if odd else both, sums_here)
                for z in range(n_z):
                    out_ref[owner * n_z + z] = block[:2, :]

    return pl.pallas_call(
        kernel,
        in_specs=[SMEM_SPEC] + [VMEM_SPEC] * (3 * quarters + 4),
        out_specs=[VMEM_SPEC] * 2,
        out_shape=[
            pltpu.VMEM((8, count), jnp.float32),
            jax.ShapeDtypeStruct((8 * n_z, 2, 2 * tok), jnp.float32),
        ],
        compiler_params=PARAMS,
        cost_estimate=cost(count, depth, cols),
    )(numbers, *[in_vmem(x) for x in (*rows, *slabs, *sums, early)])


def hessian(rows, early, late, width):
    def kernel(rows_ref, early_ref, late_ref, out_ref):
        split = early_ref.shape[1]
        total = jnp.sum(early_ref[2:3, :], axis=1, keepdims=True) + jnp.sum(
            late_ref[2:3, :], axis=1, keepdims=True
        )
        weight_early = early_ref[...].T[:, 3:4]
        weight_late = late_ref[...].T[:, 3:4]
        step = 256
        for first in range(0, width, step):
            columns = slice(first, first + step)
            x = rows_ref[:split, columns].astype(jnp.float32)
            y = rows_ref[split:, columns].astype(jnp.float32)
            value = jnp.sum(x * x * weight_early, axis=0, keepdims=True)
            value = value + jnp.sum(y * y * weight_late, axis=0, keepdims=True)
            out_ref[:, columns] = 2.0 * value / total

    return pl.pallas_call(
        kernel,
        in_specs=[VMEM_SPEC] * 3,
        out_specs=VMEM_SPEC,
        out_shape=jax.ShapeDtypeStruct((1, width), jnp.float32),
        compiler_params=PARAMS,
        cost_estimate=pl.CostEstimate(flops=4 * rows.size, bytes_accessed=2 * rows.size, transcendentals=0),
    )(rows, in_vmem(early), in_vmem(late))


def finish(numbers, back, routes, weights, n_z):
    top, tok = routes.shape

    def kernel(numbers_ref, back_ref, routes_ref, weights_ref, token_ref, expert_ref):
        own = jnp.zeros((2, 2 * tok), jnp.float32)
        err = [jnp.zeros((1, tok), jnp.float32)] * top
        power = [jnp.zeros((1, tok), jnp.float32)] * top
        for i in range(back_ref.shape[0] // n_z):
            tile = back_ref[i * n_z]
            for z in range(1, n_z):
                tile = tile + back_ref[i * n_z + z]
            own = jnp.where(numbers_ref[0] == i, tile, own)
            for k in range(top):
                here = routes_ref[k : k + 1, :] == i
                err[k] = jnp.where(here, tile[0:1, :tok], err[k])
                power[k] = jnp.where(here, tile[1:2, :tok], power[k])
        total = jnp.zeros((1, tok), jnp.float32)
        for k in range(top):
            total = total + weights_ref[k : k + 1, :] * (err[k] / (power[k] + epsilon))
        token_ref[...] = total
        expert_ref[...] = own[0:1, tok : tok + 1] / (own[1:2, tok : tok + 1] + epsilon)

    return pl.pallas_call(
        kernel,
        in_specs=[SMEM_SPEC] + [VMEM_SPEC] * 3,
        out_specs=[VMEM_SPEC] * 2,
        out_shape=[jax.ShapeDtypeStruct((1, tok), jnp.float32), jax.ShapeDtypeStruct((1, 1), jnp.float32)],
    )(numbers, in_hbm(back), in_vmem(routes), in_vmem(weights))


def in_pieces(squares):
    high = lax.reduce_precision(squares, 8, 7)
    mid = lax.reduce_precision(squares - high, 8, 7)
    return [high, mid, squares - high - mid]


def line_device(residual, attn_parts, norm_gain, routes, route_weights, w_gate, w_gate_q):
    z = lax.axis_index("tensor")
    e = lax.axis_index("expert")
    n_z = 4
    tok = residual.shape[0]
    width = residual.shape[1]

    def over_z(x, k):
        return lax.ppermute(x, "tensor", [(i, i ^ k) for i in range(n_z)])

    def in_plane(x, zero, one):
        return lax.ppermute(x, "expert", [(i, i ^ (one if i & 1 else zero)) for i in range(8)])

    def quarter(k):
        return lax.dynamic_slice(attn_parts[0], (0, (z ^ k) * width), (tok, width))

    numbers = jnp.stack([e, z, z ^ 1, z ^ 2, z ^ 3]).astype(jnp.int32)
    w, wq = w_gate[0], w_gate_q[0]

    arrived = [over_z(quarter(k), k) for k in (3, 2, 1)]
    slabs = load_product(numbers, w, wq, width)
    residual, *slabs = lax.optimization_barrier((residual, *slabs))
    hidden = residual.astype(jnp.float32) + quarter(0).astype(jnp.float32)
    for part in arrived:
        hidden = hidden + part.astype(jnp.float32)
    squares = jnp.sum(hidden * hidden, axis=1, keepdims=True)
    own = (hidden * norm_gain.astype(jnp.float32)[None, :]).astype(jnp.bfloat16)
    extra = jnp.concatenate(
        in_pieces(squares)
        + [routes.astype(jnp.float32)]
        + [jnp.full((tok, EXTRA - 3 - routes.shape[1]), -1.0, jnp.float32)],
        axis=1,
    ).astype(jnp.bfloat16)
    own = jnp.concatenate([own, extra], axis=1)
    z_near, z_far = over_z(own, 1), over_z(own, 2)
    z_both = over_z(z_far, 1)

    def other_core(rows):
        return in_plane(rows, 1, 1)

    def next_chip(rows):
        return in_plane(rows, 2, 4)

    def opposite(rows):
        return in_plane(rows, 4, 2)

    def tied(x, *values):
        return lax.optimization_barrier((x, *values))[0]

    def most(near, beside):
        return (*near, *beside, *map(other_core, beside))

    near = own, other_core(own)
    beside = next_chip(near[0]), next_chip(near[1])
    across = opposite(beside[0])
    rows = jnp.concatenate([*most(near, beside), across, other_core(across)], axis=0)
    first_sums = first_product(rows, slabs)

    def of_quarters(parts):
        return [jnp.concatenate([x[q * tok : (q + 1) * tok] for x in parts], axis=0) for q in range(2)]

    pair = tied(jnp.concatenate([z_near, z_far], axis=0), *beside)
    near = pair, other_core(pair)
    beside = next_chip(near[0]), next_chip(near[1])
    across = opposite(tied(*beside, *first_sums))
    slabs, sums = add_product(numbers, w, wq, of_quarters((*near, *beside)), width, first_sums)
    rest = of_quarters(list(map(other_core, beside)))
    last = of_quarters((across, other_core(across)))

    single = tied(z_both, beside[1])
    near = single, other_core(single)
    beside = next_chip(near[0]), next_chip(near[1])
    across = opposite(tied(*beside, *sums))
    most3 = jnp.concatenate(most(near, beside), axis=0)
    early = early_stats(numbers, most3, rest, slabs, sums, first_sums)
    last.append(jnp.concatenate([across, other_core(tied(across, early))], axis=0))
    late, payload = late_stats(numbers, last, slabs, first_sums, early, tok, n_z)

    back = lax.all_to_all(payload, ("expert", "tensor"), split_axis=0, concat_axis=0, tiled=True)
    hess = hessian(rows, early, late, width)
    token_error, expert_total = finish(numbers, back, routes.T, route_weights.T, n_z)
    return (token_error.reshape(tok), expert_total.reshape(1), hess.reshape(1, width))


def solution(mesh):
    placed = (
        P("expert", "tensor"),
        P("tensor", "expert", None),
        P("tensor"),
        P("expert", None),
        P("expert", None),
        P("expert", None, "tensor"),
        P("expert", None, "tensor"),
    )
    on_line = mesh.shape["expert"] == 8 and mesh.shape["tensor"] == 4
    return jax.shard_map(
        line_device if on_line else general_device,
        mesh=mesh,
        in_specs=placed,
        out_specs=(P("expert"), P("expert"), P("expert", "tensor")),
        check_vma=False,
    )
```

```python
import jax
import jax.numpy as jnp
from jax import lax
from jax.experimental import pallas as pl
from jax.experimental.pallas import tpu as pltpu
from jax.sharding import PartitionSpec as P

D = 7168
FF = 2048
CAP = 24
EXTRA = 128


epsilon = 1e-06


def general_device(residual, attn_parts, norm_gain, routes, route_weights, w_gate, w_gate_q):
    n_expert = lax.axis_size("expert")
    tok_count = residual.shape[0]
    local_cols = residual.shape[1]
    top_count = routes.shape[1]
    gain_wide = norm_gain.astype(jnp.float32)[None, :]
    summed = lax.psum_scatter(
        attn_parts[0].astype(jnp.float32).astype(jnp.bfloat16),
        "tensor",
        scatter_dimension=1,
        tiled=True,
    ).astype(jnp.float32)
    hidden = residual.astype(jnp.float32) + summed
    squares = lax.psum(jnp.sum(hidden * hidden, axis=1), "tensor")
    scaling = lax.rsqrt(squares / D + epsilon)
    normed = (hidden * scaling[:, None] * gain_wide).astype(jnp.bfloat16)
    expert_ids = jnp.arange(n_expert, dtype=jnp.int32)
    flat_routes = routes.reshape(-1)
    one_hot = (flat_routes[:, None] == expert_ids[None, :]).astype(jnp.int32)
    earlier = jnp.cumsum(one_hot, axis=0) - one_hot
    slot_index = jnp.sum(earlier * one_hot, axis=1)
    target = flat_routes * CAP + slot_index
    load_counts = jnp.sum(one_hot, axis=0)
    slot_ids = jnp.arange(n_expert * CAP, dtype=jnp.int32)
    placing = (slot_ids[:, None] == target[None, :]).reshape(n_expert * CAP, tok_count, top_count)
    dispatch = jnp.sum(placing.astype(jnp.int32), axis=2).astype(jnp.bfloat16)
    count_send = load_counts.astype(jnp.bfloat16).reshape(n_expert, 1)
    outgoing = jnp.dot(dispatch, normed, preferred_element_type=jnp.float32).astype(jnp.bfloat16)
    outgoing = outgoing.reshape(n_expert, CAP, local_cols)
    arrived, arrived_counts = (
        lax.all_to_all(outgoing, "expert", split_axis=0, concat_axis=0, tiled=True),
        lax.all_to_all(count_send, "expert", split_axis=0, concat_axis=0, tiled=True),
    )
    own_block = arrived.reshape(n_expert * CAP, local_cols)
    column_block = lax.all_gather(own_block, "tensor", axis=1, tiled=True)
    full_acc = jnp.dot(column_block, w_gate[0], preferred_element_type=jnp.float32)
    quant_acc = jnp.dot(column_block, w_gate_q[0], preferred_element_type=jnp.float32)
    block_squares = jnp.einsum("rc,rc->c", own_block, own_block, preferred_element_type=jnp.float32)
    total_load = jnp.sum(arrived_counts.astype(jnp.float32))
    hess_local = 2.0 * block_squares / total_load
    difference = full_acc - quant_acc
    err_part = (jnp.sum(difference * difference, axis=1) / FF).reshape(n_expert, CAP)
    pow_part = (jnp.sum(full_acc * full_acc, axis=1) / FF).reshape(n_expert, CAP)
    err_slots, pow_slots = lax.psum((err_part, pow_part), "tensor")
    expert_total = jnp.sum(err_slots) / (jnp.sum(pow_slots) + epsilon)
    back_err, back_pow = (
        lax.all_to_all(err_slots, "expert", split_axis=0, concat_axis=0, tiled=True),
        lax.all_to_all(pow_slots, "expert", split_axis=0, concat_axis=0, tiled=True),
    )
    token_err = jnp.take(back_err.reshape(-1), target).reshape(tok_count, top_count)
    token_pow = jnp.take(back_pow.reshape(-1), target).reshape(tok_count, top_count)
    ratios = token_err / (token_pow + epsilon)
    token_error = jnp.sum(route_weights * ratios, axis=1)
    return (token_error, expert_total.reshape(1), hess_local.reshape(1, local_cols))


def in_vmem(x):
    return pltpu.with_memory_space_constraint(x, pltpu.VMEM)


def in_hbm(x):
    return pltpu.with_memory_space_constraint(x, pltpu.HBM)


VMEM_SPEC = pl.BlockSpec(memory_space=pltpu.VMEM)
HBM_SPEC = pl.BlockSpec(memory_space=pl.ANY)
SMEM_SPEC = pl.BlockSpec(memory_space=pltpu.SMEM)
PARAMS = pltpu.CompilerParams(vmem_limit_bytes=24 * 1024 * 1024)


def cost(rows, depth, cols):
    return pl.CostEstimate(flops=4 * rows * depth * cols, bytes_accessed=4 * depth * cols, transcendentals=0)


def start_slab(number, hbm_ref, slab_ref, sem):
    depth = slab_ref.shape[0]
    first = pl.multiple_of(number * depth, depth)
    copy = pltpu.make_async_copy(hbm_ref.at[pl.ds(first, depth), :], slab_ref, sem)
    copy.start()
    return copy


def load_kernel(numbers_ref, w_ref, wq_ref, slab_ref, slab_q_ref, sems):
    copies = [
        start_slab(numbers_ref[1], w_ref, slab_ref, sems.at[0]),
        start_slab(numbers_ref[1], wq_ref, slab_q_ref, sems.at[1]),
    ]
    for copy in copies:
        copy.wait()


def load_product(numbers, w, wq, depth):
    return pl.pallas_call(
        load_kernel,
        in_specs=[SMEM_SPEC, HBM_SPEC, HBM_SPEC],
        out_specs=[VMEM_SPEC] * 2,
        out_shape=[pltpu.VMEM((depth, w.shape[1]), w.dtype)] * 2,
        scratch_shapes=[pltpu.SemaphoreType.DMA((2,))],
        compiler_params=PARAMS,
        cost_estimate=cost(0, depth, w.shape[1]),
    )(numbers, in_hbm(w), in_hbm(wq))


def first_product(rows, slabs):
    count = rows.shape[0]
    depth, cols = slabs[0].shape

    def kernel(rows_ref, slab_ref, slab_q_ref, full_ref, quant_ref, tail_ref):
        half = count // 2
        for part in range(2):
            here = slice(part * half, (part + 1) * half)
            x = rows_ref[here, :depth]
            full_ref[here, :] = jnp.dot(x, slab_ref[...], preferred_element_type=jnp.float32)
            quant_ref[here, :] = jnp.dot(x, slab_q_ref[...], preferred_element_type=jnp.float32)
        tail_ref[...] = rows_ref[:, depth:].astype(jnp.float32)

    return pl.pallas_call(
        kernel,
        in_specs=[VMEM_SPEC] * 3,
        out_specs=[VMEM_SPEC] * 3,
        out_shape=[pltpu.VMEM((count, cols), jnp.float32)] * 2 + [pltpu.VMEM((count, EXTRA), jnp.float32)],
        compiler_params=PARAMS,
        cost_estimate=cost(count, depth, cols),
    )(*[in_vmem(x) for x in (rows, *slabs)])


def fetching(numbers_ref, hbm_refs, slabs, sems, first):
    copies = []
    for n, slab in enumerate(slabs):
        copies.append(start_slab(numbers_ref[first + n // 2], hbm_refs[n % 2], slab, sems.at[n]))
    return copies


def add_product(numbers, w, wq, rows, depth, sums):
    count = rows[0].shape[0]
    cols = w.shape[1]
    quarters = len(rows)
    kept = 2 * quarters + 2

    def kernel(numbers_ref, w_ref, wq_ref, *refs):
        row_refs, ins, outs = refs[:quarters], refs[quarters : quarters + 3], refs[quarters + 3 : quarters + 6]
        slabs, sems = refs[quarters + 6 : -1], refs[-1]
        copies = fetching(numbers_ref, (w_ref, wq_ref), slabs, sems, 2)
        for q in range(quarters):
            for i in range(2):
                copies[2 * q + i].wait()
                before = outs[i][...] if q else ins[i][:count, :]
                outs[i][...] = before + jnp.dot(
                    row_refs[q][:, :depth], slabs[2 * q + i][...], preferred_element_type=jnp.float32
                )
        tail = ins[2][:count, :]
        for ref in row_refs:
            tail = tail + ref[:, depth:].astype(jnp.float32)
        outs[2][...] = tail
        for copy in copies[2 * quarters :]:
            copy.wait()

    out = pl.pallas_call(
        kernel,
        in_specs=[SMEM_SPEC, HBM_SPEC, HBM_SPEC] + [VMEM_SPEC] * (quarters + 3),
        out_specs=[VMEM_SPEC] * (3 + kept),
        out_shape=[pltpu.VMEM((count, cols), jnp.float32)] * 2
        + [pltpu.VMEM((count, EXTRA), jnp.float32)]
        + [pltpu.VMEM((depth, cols), w.dtype)] * kept,
        scratch_shapes=[pltpu.SemaphoreType.DMA((kept,))],
        compiler_params=PARAMS,
        cost_estimate=cost(count * quarters, depth, cols),
    )(numbers, in_hbm(w), in_hbm(wq), *[in_vmem(x) for x in (*rows, *sums)])
    return out[3:], out[:3]


def row_stats(expert, full, quant, total, extra):
    count = full.shape[0]
    diff = full - quant
    err = jnp.sum(diff * diff, axis=1, keepdims=True)
    power = jnp.sum(full * full, axis=1, keepdims=True)
    lane = lax.broadcasted_iota(jnp.int32, (count, EXTRA), 1)
    squares = total[:, 0:1] + total[:, 1:2] + total[:, 2:3]
    scale = lax.rsqrt(squares / D + epsilon)
    scale = scale * scale
    named = (lane >= 3) & (extra == expert.astype(jnp.float32))
    routed = jnp.sum(jnp.where(named, 1.0, 0.0), axis=1, keepdims=True)
    stats = jnp.where(lane == 0, err * (scale / FF), 0.0)
    stats = jnp.where(lane == 1, power * (scale / FF), stats)
    stats = jnp.where(lane == 2, routed, stats)
    stats = jnp.where(lane == 3, scale * routed, stats)
    return stats.T[:8, :]


def early_stats(numbers, rows, rest, slabs, sums, first_sums):
    count = rows.shape[0]
    done = sums[0].shape[0]
    depth, cols = slabs[0].shape
    quarters = len(rest)

    def kernel(numbers_ref, rows_ref, *refs):
        rest_refs, refs = refs[:quarters], refs[quarters:]
        slab_refs, ins, firsts, stats_ref = refs[: len(slabs)], refs[-7:-4], refs[-4:-1], refs[-1]
        expert = numbers_ref[0]
        here = slice(0, done)
        made = [
            before[...] + jnp.dot(rows_ref[here, :depth], slab[...], preferred_element_type=jnp.float32)
            for before, slab in zip(ins[:2], slab_refs[-2:])
        ]
        extra = rows_ref[here, depth:].astype(jnp.float32)
        stats_ref[:, here] = row_stats(expert, *made, ins[2][...] + extra, extra)
        here = slice(done, count)
        made = [
            before[here, :] + jnp.dot(rows_ref[here, :depth], slab[...], preferred_element_type=jnp.float32)
            for before, slab in zip(firsts[:2], slab_refs[-2:])
        ]
        extra = rows_ref[here, depth:].astype(jnp.float32)
        total = firsts[2][here, :] + extra
        for q, ref in enumerate(rest_refs):
            total = total + ref[:, depth:].astype(jnp.float32)
            for i in range(2):
                made[i] = made[i] + jnp.dot(
                    ref[:, :depth], slab_refs[2 * q + i][...], preferred_element_type=jnp.float32
                )
        stats_ref[:, here] = row_stats(expert, *made, total, extra)

    args = [rows, *rest, *slabs, *sums, *first_sums]
    return pl.pallas_call(
        kernel,
        in_specs=[SMEM_SPEC] + [VMEM_SPEC] * len(args),
        out_specs=VMEM_SPEC,
        out_shape=pltpu.VMEM((8, count), jnp.float32),
        compiler_params=PARAMS,
        cost_estimate=cost(count, depth, cols),
    )(numbers, *[in_vmem(x) for x in args])


def late_stats(numbers, rows, slabs, sums, early, tok, n_z):
    quarters = len(rows)
    count = rows[0].shape[0]
    depth, cols = slabs[0].shape

    def kernel(numbers_ref, *refs):
        row_refs, slab_refs = refs[:quarters], refs[quarters : 3 * quarters]
        full_ref, quant_ref, tail_ref, early_ref, stats_ref, out_ref = refs[3 * quarters :]
        expert = numbers_ref[0]
        core = expert % 2
        before = early_ref[...]
        here = slice(before.shape[1], before.shape[1] + count)
        total = tail_ref[here, :]
        made = [full_ref[here, :], quant_ref[here, :]]
        for q, ref in enumerate(row_refs):
            extra = ref[:, depth:].astype(jnp.float32)
            total = total + extra
            for i in range(2):
                made[i] = made[i] + jnp.dot(
                    ref[:, :depth], slab_refs[2 * q + i][...], preferred_element_type=jnp.float32
                )
        stats = row_stats(expert, *made, total, extra)
        stats_ref[...] = stats
        sums_early = jnp.sum(before * before[2:3, :], axis=1, keepdims=True)
        sums_here = sums_early + jnp.sum(stats * stats[2:3, :], axis=1, keepdims=True)
        lane = lax.broadcasted_iota(jnp.int32, (8, 2 * tok), 1)
        order = ((0, 0), (1, 1), (2, 4), (3, 5), (5, 3), (4, 2), (6, 6), (7, 7))
        for pair in range(4):
            both = stats if pair == 3 else before[:, pair * 2 * tok : (pair + 1) * 2 * tok]
            for odd in range(2):
                zero, one = order[2 * pair + odd]
                owner = expert ^ (zero + core * (one - zero))
                block = jnp.where(lane < tok, pltpu.roll(both, tok, 1) if odd else both, sums_here)
                for z in range(n_z):
                    out_ref[owner * n_z + z] = block[:2, :]

    return pl.pallas_call(
        kernel,
        in_specs=[SMEM_SPEC] + [VMEM_SPEC] * (3 * quarters + 4),
        out_specs=[VMEM_SPEC] * 2,
        out_shape=[
            pltpu.VMEM((8, count), jnp.float32),
            jax.ShapeDtypeStruct((8 * n_z, 2, 2 * tok), jnp.float32),
        ],
        compiler_params=PARAMS,
        cost_estimate=cost(count, depth, cols),
    )(numbers, *[in_vmem(x) for x in (*rows, *slabs, *sums, early)])


def hessian(rows, early, late, width):
    def kernel(rows_ref, early_ref, late_ref, out_ref):
        split = early_ref.shape[1]
        total = jnp.sum(early_ref[2:3, :], axis=1, keepdims=True) + jnp.sum(
            late_ref[2:3, :], axis=1, keepdims=True
        )
        weight_early = early_ref[...].T[:, 3:4]
        weight_late = late_ref[...].T[:, 3:4]
        step = 256
        for first in range(0, width, step):
            columns = slice(first, first + step)
            x = rows_ref[:split, columns].astype(jnp.float32)
            y = rows_ref[split:, columns].astype(jnp.float32)
            value = jnp.sum(x * x * weight_early, axis=0, keepdims=True)
            value = value + jnp.sum(y * y * weight_late, axis=0, keepdims=True)
            out_ref[:, columns] = 2.0 * value / total

    return pl.pallas_call(
        kernel,
        in_specs=[VMEM_SPEC] * 3,
        out_specs=VMEM_SPEC,
        out_shape=jax.ShapeDtypeStruct((1, width), jnp.float32),
        compiler_params=PARAMS,
        cost_estimate=pl.CostEstimate(flops=4 * rows.size, bytes_accessed=2 * rows.size, transcendentals=0),
    )(rows, in_vmem(early), in_vmem(late))


def finish(numbers, back, routes, weights, n_z):
    top, tok = routes.shape

    def kernel(numbers_ref, back_ref, routes_ref, weights_ref, token_ref, expert_ref):
        own = jnp.zeros((2, 2 * tok), jnp.float32)
        err = [jnp.zeros((1, tok), jnp.float32)] * top
        power = [jnp.zeros((1, tok), jnp.float32)] * top
        for i in range(back_ref.shape[0] // n_z):
            tile = back_ref[i * n_z]
            for z in range(1, n_z):
                tile = tile + back_ref[i * n_z + z]
            own = jnp.where(numbers_ref[0] == i, tile, own)
            for k in range(top):
                here = routes_ref[k : k + 1, :] == i
                err[k] = jnp.where(here, tile[0:1, :tok], err[k])
                power[k] = jnp.where(here, tile[1:2, :tok], power[k])
        total = jnp.zeros((1, tok), jnp.float32)
        for k in range(top):
            total = total + weights_ref[k : k + 1, :] * (err[k] / (power[k] + epsilon))
        token_ref[...] = total
        expert_ref[...] = own[0:1, tok : tok + 1] / (own[1:2, tok : tok + 1] + epsilon)

    return pl.pallas_call(
        kernel,
        in_specs=[SMEM_SPEC] + [VMEM_SPEC] * 3,
        out_specs=[VMEM_SPEC] * 2,
        out_shape=[jax.ShapeDtypeStruct((1, tok), jnp.float32), jax.ShapeDtypeStruct((1, 1), jnp.float32)],
    )(numbers, in_hbm(back), in_vmem(routes), in_vmem(weights))


def in_pieces(squares):
    high = lax.reduce_precision(squares, 8, 7)
    mid = lax.reduce_precision(squares - high, 8, 7)
    return [high, mid, squares - high - mid]


def line_device(residual, attn_parts, norm_gain, routes, route_weights, w_gate, w_gate_q):
    z = lax.axis_index("tensor")
    e = lax.axis_index("expert")
    n_z = 4
    tok = residual.shape[0]
    width = residual.shape[1]

    def over_z(x, k):
        return lax.ppermute(x, "tensor", [(i, i ^ k) for i in range(n_z)])

    def in_plane(x, zero, one):
        return lax.ppermute(x, "expert", [(i, i ^ (one if i & 1 else zero)) for i in range(8)])

    def quarter(k):
        return lax.dynamic_slice(attn_parts[0], (0, (z ^ k) * width), (tok, width))

    numbers = jnp.stack([e, z, z ^ 1, z ^ 2, z ^ 3]).astype(jnp.int32)
    w, wq = w_gate[0], w_gate_q[0]

    arrived = [over_z(quarter(k), k) for k in (3, 2, 1)]
    slabs = load_product(numbers, w, wq, width)
    residual, *slabs = lax.optimization_barrier((residual, *slabs))
    hidden = residual.astype(jnp.float32) + quarter(0).astype(jnp.float32)
    for part in arrived:
        hidden = hidden + part.astype(jnp.float32)
    squares = jnp.sum(hidden * hidden, axis=1, keepdims=True)
    own = (hidden * norm_gain.astype(jnp.float32)[None, :]).astype(jnp.bfloat16)
    extra = jnp.concatenate(
        in_pieces(squares)
        + [routes.astype(jnp.float32)]
        + [jnp.full((tok, EXTRA - 3 - routes.shape[1]), -1.0, jnp.float32)],
        axis=1,
    ).astype(jnp.bfloat16)
    own = jnp.concatenate([own, extra], axis=1)
    z_near, z_far = over_z(own, 1), over_z(own, 2)
    z_both = over_z(z_far, 1)

    def other_core(rows):
        return in_plane(rows, 1, 1)

    def next_chip(rows):
        return in_plane(rows, 2, 4)

    def opposite(rows):
        return in_plane(rows, 4, 2)

    def tied(x, *values):
        return lax.optimization_barrier((x, *values))[0]

    near = own, other_core(own)
    beside_x = next_chip(near[0])
    beside = beside_x, next_chip(tied(near[1], beside_x))
    across = opposite(beside[0])
    rows = jnp.concatenate([*near, *beside, *map(other_core, beside), across, other_core(across)], axis=0)
    first_sums = first_product(rows, slabs)
    across_far = over_z(across, 2)

    def of_quarters(parts):
        return [jnp.concatenate([x[q * tok : (q + 1) * tok] for x in parts], axis=0) for q in range(2)]

    pair = tied(jnp.concatenate([z_near, z_far], axis=0), *beside)
    near = pair, other_core(pair)
    beside = next_chip(near[0]), next_chip(near[1])
    across = opposite(tied(beside[0], beside[1], *first_sums))
    ready = of_quarters((*near, *beside))
    ready[0] = tied(ready[0], z_both)
    slabs, sums = add_product(numbers, w, wq, ready, width, first_sums)
    rest = of_quarters([other_core(x) for x in beside])
    last = of_quarters((across, other_core(across)))

    single = tied(z_both, beside[1])
    across_far = tied(across_far, beside[1])
    near = single, other_core(single)
    beside = next_chip(near[0]), next_chip(near[1])
    across = over_z(across_far, 1)
    most = jnp.concatenate([*near, *beside, *map(other_core, beside)], axis=0)
    early = early_stats(numbers, most, rest, slabs, sums, first_sums)
    last.append(jnp.concatenate([across, other_core(across)], axis=0))
    late, payload = late_stats(numbers, last, slabs, first_sums, early, tok, n_z)

    back = lax.all_to_all(payload, ("expert", "tensor"), split_axis=0, concat_axis=0, tiled=True)
    hess = hessian(rows, early, late, width)
    token_error, expert_total = finish(numbers, back, routes.T, route_weights.T, n_z)
    return (token_error.reshape(tok), expert_total.reshape(1), hess.reshape(1, width))


def solution(mesh):
    placed = (
        P("expert", "tensor"),
        P("tensor", "expert", None),
        P("tensor"),
        P("expert", None),
        P("expert", None),
        P("expert", None, "tensor"),
        P("expert", None, "tensor"),
    )
    on_line = mesh.shape["expert"] == 8 and mesh.shape["tensor"] == 4
    return jax.shard_map(
        line_device if on_line else general_device,
        mesh=mesh,
        in_specs=placed,
        out_specs=(P("expert"), P("expert"), P("expert", "tensor")),
        check_vma=False,
    )
```

```python
import jax
import jax.numpy as jnp
from jax import lax
from jax.experimental import pallas as pl
from jax.experimental.pallas import tpu as pltpu
from jax.sharding import PartitionSpec as P

D = 7168
FF = 2048
CAP = 24
EXTRA = 128


epsilon = 1e-06


def general_device(residual, attn_parts, norm_gain, routes, route_weights, w_gate, w_gate_q):
    n_expert = lax.axis_size("expert")
    tok_count = residual.shape[0]
    local_cols = residual.shape[1]
    top_count = routes.shape[1]
    gain_wide = norm_gain.astype(jnp.float32)[None, :]
    summed = lax.psum_scatter(
        attn_parts[0].astype(jnp.float32).astype(jnp.bfloat16),
        "tensor",
        scatter_dimension=1,
        tiled=True,
    ).astype(jnp.float32)
    hidden = residual.astype(jnp.float32) + summed
    squares = lax.psum(jnp.sum(hidden * hidden, axis=1), "tensor")
    scaling = lax.rsqrt(squares / D + epsilon)
    normed = (hidden * scaling[:, None] * gain_wide).astype(jnp.bfloat16)
    expert_ids = jnp.arange(n_expert, dtype=jnp.int32)
    flat_routes = routes.reshape(-1)
    one_hot = (flat_routes[:, None] == expert_ids[None, :]).astype(jnp.int32)
    earlier = jnp.cumsum(one_hot, axis=0) - one_hot
    slot_index = jnp.sum(earlier * one_hot, axis=1)
    target = flat_routes * CAP + slot_index
    load_counts = jnp.sum(one_hot, axis=0)
    slot_ids = jnp.arange(n_expert * CAP, dtype=jnp.int32)
    placing = (slot_ids[:, None] == target[None, :]).reshape(n_expert * CAP, tok_count, top_count)
    dispatch = jnp.sum(placing.astype(jnp.int32), axis=2).astype(jnp.bfloat16)
    count_send = load_counts.astype(jnp.bfloat16).reshape(n_expert, 1)
    outgoing = jnp.dot(dispatch, normed, preferred_element_type=jnp.float32).astype(jnp.bfloat16)
    outgoing = outgoing.reshape(n_expert, CAP, local_cols)
    arrived, arrived_counts = (
        lax.all_to_all(outgoing, "expert", split_axis=0, concat_axis=0, tiled=True),
        lax.all_to_all(count_send, "expert", split_axis=0, concat_axis=0, tiled=True),
    )
    own_block = arrived.reshape(n_expert * CAP, local_cols)
    column_block = lax.all_gather(own_block, "tensor", axis=1, tiled=True)
    full_acc = jnp.dot(column_block, w_gate[0], preferred_element_type=jnp.float32)
    quant_acc = jnp.dot(column_block, w_gate_q[0], preferred_element_type=jnp.float32)
    block_squares = jnp.einsum("rc,rc->c", own_block, own_block, preferred_element_type=jnp.float32)
    total_load = jnp.sum(arrived_counts.astype(jnp.float32))
    hess_local = 2.0 * block_squares / total_load
    difference = full_acc - quant_acc
    err_part = (jnp.sum(difference * difference, axis=1) / FF).reshape(n_expert, CAP)
    pow_part = (jnp.sum(full_acc * full_acc, axis=1) / FF).reshape(n_expert, CAP)
    err_slots, pow_slots = lax.psum((err_part, pow_part), "tensor")
    expert_total = jnp.sum(err_slots) / (jnp.sum(pow_slots) + epsilon)
    back_err, back_pow = (
        lax.all_to_all(err_slots, "expert", split_axis=0, concat_axis=0, tiled=True),
        lax.all_to_all(pow_slots, "expert", split_axis=0, concat_axis=0, tiled=True),
    )
    token_err = jnp.take(back_err.reshape(-1), target).reshape(tok_count, top_count)
    token_pow = jnp.take(back_pow.reshape(-1), target).reshape(tok_count, top_count)
    ratios = token_err / (token_pow + epsilon)
    token_error = jnp.sum(route_weights * ratios, axis=1)
    return (token_error, expert_total.reshape(1), hess_local.reshape(1, local_cols))


def in_vmem(x):
    return pltpu.with_memory_space_constraint(x, pltpu.VMEM)


def in_hbm(x):
    return pltpu.with_memory_space_constraint(x, pltpu.HBM)


VMEM_SPEC = pl.BlockSpec(memory_space=pltpu.VMEM)
HBM_SPEC = pl.BlockSpec(memory_space=pl.ANY)
SMEM_SPEC = pl.BlockSpec(memory_space=pltpu.SMEM)
PARAMS = pltpu.CompilerParams(vmem_limit_bytes=24 * 1024 * 1024)


def cost(rows, depth, cols):
    return pl.CostEstimate(flops=4 * rows * depth * cols, bytes_accessed=4 * depth * cols, transcendentals=0)


def start_slab(number, hbm_ref, slab_ref, sem):
    depth = slab_ref.shape[0]
    first = pl.multiple_of(number * depth, depth)
    copy = pltpu.make_async_copy(hbm_ref.at[pl.ds(first, depth), :], slab_ref, sem)
    copy.start()
    return copy


def load_kernel(numbers_ref, w_ref, wq_ref, slab_ref, slab_q_ref, sems):
    copies = [
        start_slab(numbers_ref[1], w_ref, slab_ref, sems.at[0]),
        start_slab(numbers_ref[1], wq_ref, slab_q_ref, sems.at[1]),
    ]
    for copy in copies:
        copy.wait()


def load_product(numbers, w, wq, depth):
    return pl.pallas_call(
        load_kernel,
        in_specs=[SMEM_SPEC, HBM_SPEC, HBM_SPEC],
        out_specs=[VMEM_SPEC] * 2,
        out_shape=[pltpu.VMEM((depth, w.shape[1]), w.dtype)] * 2,
        scratch_shapes=[pltpu.SemaphoreType.DMA((2,))],
        compiler_params=PARAMS,
        cost_estimate=cost(0, depth, w.shape[1]),
    )(numbers, in_hbm(w), in_hbm(wq))


def first_product(rows, slabs):
    count = rows.shape[0]
    depth, cols = slabs[0].shape

    def kernel(rows_ref, slab_ref, slab_q_ref, full_ref, quant_ref, tail_ref):
        half = count // 2
        for part in range(2):
            here = slice(part * half, (part + 1) * half)
            x = rows_ref[here, :depth]
            full_ref[here, :] = jnp.dot(x, slab_ref[...], preferred_element_type=jnp.float32)
            quant_ref[here, :] = jnp.dot(x, slab_q_ref[...], preferred_element_type=jnp.float32)
        tail_ref[...] = rows_ref[:, depth:].astype(jnp.float32)

    return pl.pallas_call(
        kernel,
        in_specs=[VMEM_SPEC] * 3,
        out_specs=[VMEM_SPEC] * 3,
        out_shape=[pltpu.VMEM((count, cols), jnp.float32)] * 2 + [pltpu.VMEM((count, EXTRA), jnp.float32)],
        compiler_params=PARAMS,
        cost_estimate=cost(count, depth, cols),
    )(*[in_vmem(x) for x in (rows, *slabs)])


def fetching(numbers_ref, hbm_refs, slabs, sems, first):
    copies = []
    for n, slab in enumerate(slabs):
        copies.append(start_slab(numbers_ref[first + n // 2], hbm_refs[n % 2], slab, sems.at[n]))
    return copies


def add_product(numbers, w, wq, rows, depth, sums):
    count = rows[0].shape[0]
    cols = w.shape[1]
    quarters = len(rows)
    kept = 2 * quarters + 2

    def kernel(numbers_ref, w_ref, wq_ref, *refs):
        row_refs, ins, outs = refs[:quarters], refs[quarters : quarters + 3], refs[quarters + 3 : quarters + 6]
        slabs, sems = refs[quarters + 6 : -1], refs[-1]
        copies = fetching(numbers_ref, (w_ref, wq_ref), slabs, sems, 2)
        for q in range(quarters):
            for i in range(2):
                copies[2 * q + i].wait()
                before = outs[i][...] if q else ins[i][:count, :]
                outs[i][...] = before + jnp.dot(
                    row_refs[q][:, :depth], slabs[2 * q + i][...], preferred_element_type=jnp.float32
                )
        tail = ins[2][:count, :]
        for ref in row_refs:
            tail = tail + ref[:, depth:].astype(jnp.float32)
        outs[2][...] = tail
        for copy in copies[2 * quarters :]:
            copy.wait()

    out = pl.pallas_call(
        kernel,
        in_specs=[SMEM_SPEC, HBM_SPEC, HBM_SPEC] + [VMEM_SPEC] * (quarters + 3),
        out_specs=[VMEM_SPEC] * (3 + kept),
        out_shape=[pltpu.VMEM((count, cols), jnp.float32)] * 2
        + [pltpu.VMEM((count, EXTRA), jnp.float32)]
        + [pltpu.VMEM((depth, cols), w.dtype)] * kept,
        scratch_shapes=[pltpu.SemaphoreType.DMA((kept,))],
        compiler_params=PARAMS,
        cost_estimate=cost(count * quarters, depth, cols),
    )(numbers, in_hbm(w), in_hbm(wq), *[in_vmem(x) for x in (*rows, *sums)])
    return out[3:], out[:3]


def row_stats(expert, full, quant, total, extra):
    count = full.shape[0]
    diff = full - quant
    err = jnp.sum(diff * diff, axis=1, keepdims=True)
    power = jnp.sum(full * full, axis=1, keepdims=True)
    lane = lax.broadcasted_iota(jnp.int32, (count, EXTRA), 1)
    squares = total[:, 0:1] + total[:, 1:2] + total[:, 2:3]
    scale = lax.rsqrt(squares / D + epsilon)
    scale = scale * scale
    named = (lane >= 3) & (extra == expert.astype(jnp.float32))
    routed = jnp.sum(jnp.where(named, 1.0, 0.0), axis=1, keepdims=True)
    stats = jnp.where(lane == 0, err * (scale / FF), 0.0)
    stats = jnp.where(lane == 1, power * (scale / FF), stats)
    stats = jnp.where(lane == 2, routed, stats)
    stats = jnp.where(lane == 3, scale * routed, stats)
    return stats.T[:8, :]


def early_stats(numbers, rows, rest, slabs, sums, first_sums):
    count = rows.shape[0]
    done = sums[0].shape[0]
    depth, cols = slabs[0].shape
    quarters = len(rest)

    def kernel(numbers_ref, rows_ref, *refs):
        rest_refs, refs = refs[:quarters], refs[quarters:]
        slab_refs, ins, firsts, stats_ref = refs[: len(slabs)], refs[-7:-4], refs[-4:-1], refs[-1]
        expert = numbers_ref[0]
        here = slice(0, done)
        made = [
            before[...] + jnp.dot(rows_ref[here, :depth], slab[...], preferred_element_type=jnp.float32)
            for before, slab in zip(ins[:2], slab_refs[-2:])
        ]
        extra = rows_ref[here, depth:].astype(jnp.float32)
        stats_ref[:, here] = row_stats(expert, *made, ins[2][...] + extra, extra)
        here = slice(done, count)
        made = [
            before[here, :] + jnp.dot(rows_ref[here, :depth], slab[...], preferred_element_type=jnp.float32)
            for before, slab in zip(firsts[:2], slab_refs[-2:])
        ]
        extra = rows_ref[here, depth:].astype(jnp.float32)
        total = firsts[2][here, :] + extra
        for q, ref in enumerate(rest_refs):
            total = total + ref[:, depth:].astype(jnp.float32)
            for i in range(2):
                made[i] = made[i] + jnp.dot(
                    ref[:, :depth], slab_refs[2 * q + i][...], preferred_element_type=jnp.float32
                )
        stats_ref[:, here] = row_stats(expert, *made, total, extra)

    args = [rows, *rest, *slabs, *sums, *first_sums]
    return pl.pallas_call(
        kernel,
        in_specs=[SMEM_SPEC] + [VMEM_SPEC] * len(args),
        out_specs=VMEM_SPEC,
        out_shape=pltpu.VMEM((8, count), jnp.float32),
        compiler_params=PARAMS,
        cost_estimate=cost(count, depth, cols),
    )(numbers, *[in_vmem(x) for x in args])


def late_stats(numbers, rows, slabs, sums, early, tok, n_z):
    quarters = len(rows)
    count = rows[0].shape[0]
    depth, cols = slabs[0].shape

    def kernel(numbers_ref, *refs):
        row_refs, slab_refs = refs[:quarters], refs[quarters : 3 * quarters]
        full_ref, quant_ref, tail_ref, early_ref, stats_ref, out_ref = refs[3 * quarters :]
        expert = numbers_ref[0]
        core = expert % 2
        before = early_ref[...]
        here = slice(before.shape[1], before.shape[1] + count)
        total = tail_ref[here, :]
        made = [full_ref[here, :], quant_ref[here, :]]
        for q, ref in enumerate(row_refs):
            extra = ref[:, depth:].astype(jnp.float32)
            total = total + extra
            for i in range(2):
                made[i] = made[i] + jnp.dot(
                    ref[:, :depth], slab_refs[2 * q + i][...], preferred_element_type=jnp.float32
                )
        stats = row_stats(expert, *made, total, extra)
        stats_ref[...] = stats
        sums_early = jnp.sum(before * before[2:3, :], axis=1, keepdims=True)
        sums_here = sums_early + jnp.sum(stats * stats[2:3, :], axis=1, keepdims=True)
        lane = lax.broadcasted_iota(jnp.int32, (8, 2 * tok), 1)
        order = ((0, 0), (1, 1), (2, 4), (3, 5), (5, 3), (4, 2), (6, 6), (7, 7))
        for pair in range(4):
            both = stats if pair == 3 else before[:, pair * 2 * tok : (pair + 1) * 2 * tok]
            for odd in range(2):
                zero, one = order[2 * pair + odd]
                owner = expert ^ (zero + core * (one - zero))
                block = jnp.where(lane < tok, pltpu.roll(both, tok, 1) if odd else both, sums_here)
                for z in range(n_z):
                    out_ref[owner * n_z + z] = block[:2, :]

    return pl.pallas_call(
        kernel,
        in_specs=[SMEM_SPEC] + [VMEM_SPEC] * (3 * quarters + 4),
        out_specs=[VMEM_SPEC] * 2,
        out_shape=[
            pltpu.VMEM((8, count), jnp.float32),
            jax.ShapeDtypeStruct((8 * n_z, 2, 2 * tok), jnp.float32),
        ],
        compiler_params=PARAMS,
        cost_estimate=cost(count, depth, cols),
    )(numbers, *[in_vmem(x) for x in (*rows, *slabs, *sums, early)])


def hessian(rows, early, late, width):
    def kernel(rows_ref, early_ref, late_ref, out_ref):
        split = early_ref.shape[1]
        total = jnp.sum(early_ref[2:3, :], axis=1, keepdims=True) + jnp.sum(
            late_ref[2:3, :], axis=1, keepdims=True
        )
        weight_early = early_ref[...].T[:, 3:4]
        weight_late = late_ref[...].T[:, 3:4]
        step = 256
        for first in range(0, width, step):
            columns = slice(first, first + step)
            x = rows_ref[:split, columns].astype(jnp.float32)
            y = rows_ref[split:, columns].astype(jnp.float32)
            value = jnp.sum(x * x * weight_early, axis=0, keepdims=True)
            value = value + jnp.sum(y * y * weight_late, axis=0, keepdims=True)
            out_ref[:, columns] = 2.0 * value / total

    return pl.pallas_call(
        kernel,
        in_specs=[VMEM_SPEC] * 3,
        out_specs=VMEM_SPEC,
        out_shape=jax.ShapeDtypeStruct((1, width), jnp.float32),
        compiler_params=PARAMS,
        cost_estimate=pl.CostEstimate(flops=4 * rows.size, bytes_accessed=2 * rows.size, transcendentals=0),
    )(rows, in_vmem(early), in_vmem(late))


def finish(numbers, back, routes, weights, n_z):
    top, tok = routes.shape

    def kernel(numbers_ref, back_ref, routes_ref, weights_ref, token_ref, expert_ref):
        own = jnp.zeros((2, 2 * tok), jnp.float32)
        err = [jnp.zeros((1, tok), jnp.float32)] * top
        power = [jnp.zeros((1, tok), jnp.float32)] * top
        for i in range(back_ref.shape[0] // n_z):
            tile = back_ref[i * n_z]
            for z in range(1, n_z):
                tile = tile + back_ref[i * n_z + z]
            own = jnp.where(numbers_ref[0] == i, tile, own)
            for k in range(top):
                here = routes_ref[k : k + 1, :] == i
                err[k] = jnp.where(here, tile[0:1, :tok], err[k])
                power[k] = jnp.where(here, tile[1:2, :tok], power[k])
        total = jnp.zeros((1, tok), jnp.float32)
        for k in range(top):
            total = total + weights_ref[k : k + 1, :] * (err[k] / (power[k] + epsilon))
        token_ref[...] = total
        expert_ref[...] = own[0:1, tok : tok + 1] / (own[1:2, tok : tok + 1] + epsilon)

    return pl.pallas_call(
        kernel,
        in_specs=[SMEM_SPEC] + [VMEM_SPEC] * 3,
        out_specs=[VMEM_SPEC] * 2,
        out_shape=[jax.ShapeDtypeStruct((1, tok), jnp.float32), jax.ShapeDtypeStruct((1, 1), jnp.float32)],
    )(numbers, in_vmem(back), routes, weights)


def in_pieces(squares):
    high = lax.reduce_precision(squares, 8, 7)
    mid = lax.reduce_precision(squares - high, 8, 7)
    return [high, mid, squares - high - mid]


def line_device(residual, attn_parts, norm_gain, routes, route_weights, w_gate, w_gate_q):
    z = lax.axis_index("tensor")
    e = lax.axis_index("expert")
    n_z = 4
    tok = residual.shape[0]
    width = residual.shape[1]

    def over_z(x, k):
        return lax.ppermute(x, "tensor", [(i, i ^ k) for i in range(n_z)])

    def in_plane(x, zero, one):
        return lax.ppermute(x, "expert", [(i, i ^ (one if i & 1 else zero)) for i in range(8)])

    def quarter(k):
        return lax.dynamic_slice(attn_parts[0], (0, (z ^ k) * width), (tok, width))

    numbers = jnp.stack([e, z, z ^ 1, z ^ 2, z ^ 3]).astype(jnp.int32)
    w, wq = w_gate[0], w_gate_q[0]

    arrived = [over_z(quarter(k), k) for k in (3, 2, 1)]
    slabs = load_product(numbers, w, wq, width)
    residual, *slabs = lax.optimization_barrier((residual, *slabs))
    hidden = residual.astype(jnp.float32) + quarter(0).astype(jnp.float32)
    for part in arrived:
        hidden = hidden + part.astype(jnp.float32)
    squares = jnp.sum(hidden * hidden, axis=1, keepdims=True)
    own = (hidden * norm_gain.astype(jnp.float32)[None, :]).astype(jnp.bfloat16)
    extra = jnp.concatenate(
        in_pieces(squares)
        + [routes.astype(jnp.float32)]
        + [jnp.full((tok, EXTRA - 3 - routes.shape[1]), -1.0, jnp.float32)],
        axis=1,
    ).astype(jnp.bfloat16)
    own = jnp.concatenate([own, extra], axis=1)
    z_near, z_far = over_z(own, 1), over_z(own, 2)
    z_both = over_z(z_far, 1)

    def other_core(rows):
        return in_plane(rows, 1, 1)

    def next_chip(rows):
        return in_plane(rows, 2, 4)

    def opposite(rows):
        return in_plane(rows, 4, 2)

    def tied(x, *values):
        return lax.optimization_barrier((x, *values))[0]

    near = own, other_core(own)
    beside_x = next_chip(near[0])
    beside = beside_x, next_chip(tied(near[1], beside_x))
    across = opposite(beside[0])
    rows = jnp.concatenate([*near, *beside, *map(other_core, beside), across, other_core(across)], axis=0)
    first_sums = first_product(rows, slabs)
    across_far = over_z(across, 2)

    def of_quarters(parts):
        return [jnp.concatenate([x[q * tok : (q + 1) * tok] for x in parts], axis=0) for q in range(2)]

    pair = tied(jnp.concatenate([z_near, z_far], axis=0), *beside)
    near = pair, other_core(pair)
    beside = next_chip(near[0]), next_chip(near[1])
    across = opposite(tied(beside[0], beside[1], *first_sums))
    ready = of_quarters((*near, *beside))
    ready[0] = tied(ready[0], z_both)
    slabs, sums = add_product(numbers, w, wq, ready, width, first_sums)
    rest = of_quarters([other_core(x) for x in beside])
    last = of_quarters((across, other_core(across)))

    single = tied(z_both, beside[1])
    across_far = tied(across_far, beside[1])
    near = single, other_core(single)
    beside = next_chip(near[0]), next_chip(near[1])
    across = over_z(across_far, 1)
    most = jnp.concatenate([*near, *beside, *map(other_core, beside)], axis=0)
    early = early_stats(numbers, most, rest, slabs, sums, first_sums)
    last.append(jnp.concatenate([across, other_core(across)], axis=0))
    late, payload = late_stats(numbers, last, slabs, first_sums, early, tok, n_z)

    back = lax.all_to_all(payload, ("expert", "tensor"), split_axis=0, concat_axis=0, tiled=True)
    hess = hessian(rows, early, late, width)
    token_error, expert_total = finish(numbers, back, routes.T, route_weights.T, n_z)
    return (token_error.reshape(tok), expert_total.reshape(1), hess.reshape(1, width))


def solution(mesh):
    placed = (
        P("expert", "tensor"),
        P("tensor", "expert", None),
        P("tensor"),
        P("expert", None),
        P("expert", None),
        P("expert", None, "tensor"),
        P("expert", None, "tensor"),
    )
    on_line = mesh.shape["expert"] == 8 and mesh.shape["tensor"] == 4
    return jax.shard_map(
        line_device if on_line else general_device,
        mesh=mesh,
        in_specs=placed,
        out_specs=(P("expert"), P("expert"), P("expert", "tensor")),
        check_vma=False,
    )
```

```python
import jax
import jax.numpy as jnp
from jax import lax
from jax.experimental import pallas as pl
from jax.experimental.pallas import tpu as pltpu
from jax.sharding import PartitionSpec as P

D = 7168
FF = 2048
CAP = 24
EXTRA = 128


epsilon = 1e-06


def general_device(residual, attn_parts, norm_gain, routes, route_weights, w_gate, w_gate_q):
    n_expert = lax.axis_size("expert")
    tok_count = residual.shape[0]
    local_cols = residual.shape[1]
    top_count = routes.shape[1]
    gain_wide = norm_gain.astype(jnp.float32)[None, :]
    summed = lax.psum_scatter(
        attn_parts[0].astype(jnp.float32).astype(jnp.bfloat16),
        "tensor",
        scatter_dimension=1,
        tiled=True,
    ).astype(jnp.float32)
    hidden = residual.astype(jnp.float32) + summed
    squares = lax.psum(jnp.sum(hidden * hidden, axis=1), "tensor")
    scaling = lax.rsqrt(squares / D + epsilon)
    normed = (hidden * scaling[:, None] * gain_wide).astype(jnp.bfloat16)
    expert_ids = jnp.arange(n_expert, dtype=jnp.int32)
    flat_routes = routes.reshape(-1)
    one_hot = (flat_routes[:, None] == expert_ids[None, :]).astype(jnp.int32)
    earlier = jnp.cumsum(one_hot, axis=0) - one_hot
    slot_index = jnp.sum(earlier * one_hot, axis=1)
    target = flat_routes * CAP + slot_index
    load_counts = jnp.sum(one_hot, axis=0)
    slot_ids = jnp.arange(n_expert * CAP, dtype=jnp.int32)
    placing = (slot_ids[:, None] == target[None, :]).reshape(n_expert * CAP, tok_count, top_count)
    dispatch = jnp.sum(placing.astype(jnp.int32), axis=2).astype(jnp.bfloat16)
    count_send = load_counts.astype(jnp.bfloat16).reshape(n_expert, 1)
    outgoing = jnp.dot(dispatch, normed, preferred_element_type=jnp.float32).astype(jnp.bfloat16)
    outgoing = outgoing.reshape(n_expert, CAP, local_cols)
    arrived, arrived_counts = (
        lax.all_to_all(outgoing, "expert", split_axis=0, concat_axis=0, tiled=True),
        lax.all_to_all(count_send, "expert", split_axis=0, concat_axis=0, tiled=True),
    )
    own_block = arrived.reshape(n_expert * CAP, local_cols)
    column_block = lax.all_gather(own_block, "tensor", axis=1, tiled=True)
    full_acc = jnp.dot(column_block, w_gate[0], preferred_element_type=jnp.float32)
    quant_acc = jnp.dot(column_block, w_gate_q[0], preferred_element_type=jnp.float32)
    block_squares = jnp.einsum("rc,rc->c", own_block, own_block, preferred_element_type=jnp.float32)
    total_load = jnp.sum(arrived_counts.astype(jnp.float32))
    hess_local = 2.0 * block_squares / total_load
    difference = full_acc - quant_acc
    err_part = (jnp.sum(difference * difference, axis=1) / FF).reshape(n_expert, CAP)
    pow_part = (jnp.sum(full_acc * full_acc, axis=1) / FF).reshape(n_expert, CAP)
    err_slots, pow_slots = lax.psum((err_part, pow_part), "tensor")
    expert_total = jnp.sum(err_slots) / (jnp.sum(pow_slots) + epsilon)
    back_err, back_pow = (
        lax.all_to_all(err_slots, "expert", split_axis=0, concat_axis=0, tiled=True),
        lax.all_to_all(pow_slots, "expert", split_axis=0, concat_axis=0, tiled=True),
    )
    token_err = jnp.take(back_err.reshape(-1), target).reshape(tok_count, top_count)
    token_pow = jnp.take(back_pow.reshape(-1), target).reshape(tok_count, top_count)
    ratios = token_err / (token_pow + epsilon)
    token_error = jnp.sum(route_weights * ratios, axis=1)
    return (token_error, expert_total.reshape(1), hess_local.reshape(1, local_cols))


def in_vmem(x):
    return pltpu.with_memory_space_constraint(x, pltpu.VMEM)


def in_hbm(x):
    return pltpu.with_memory_space_constraint(x, pltpu.HBM)


VMEM_SPEC = pl.BlockSpec(memory_space=pltpu.VMEM)
HBM_SPEC = pl.BlockSpec(memory_space=pl.ANY)
SMEM_SPEC = pl.BlockSpec(memory_space=pltpu.SMEM)
PARAMS = pltpu.CompilerParams(vmem_limit_bytes=24 * 1024 * 1024)


def cost(rows, depth, cols):
    return pl.CostEstimate(flops=4 * rows * depth * cols, bytes_accessed=4 * depth * cols, transcendentals=0)


def start_slab(number, hbm_ref, slab_ref, sem):
    depth = slab_ref.shape[0]
    first = pl.multiple_of(number * depth, depth)
    copy = pltpu.make_async_copy(hbm_ref.at[pl.ds(first, depth), :], slab_ref, sem)
    copy.start()
    return copy


def load_kernel(numbers_ref, w_ref, wq_ref, slab_ref, slab_q_ref, sems):
    copies = [
        start_slab(numbers_ref[1], w_ref, slab_ref, sems.at[0]),
        start_slab(numbers_ref[1], wq_ref, slab_q_ref, sems.at[1]),
    ]
    for copy in copies:
        copy.wait()


def load_product(numbers, w, wq, depth):
    return pl.pallas_call(
        load_kernel,
        in_specs=[SMEM_SPEC, HBM_SPEC, HBM_SPEC],
        out_specs=[VMEM_SPEC] * 2,
        out_shape=[pltpu.VMEM((depth, w.shape[1]), w.dtype)] * 2,
        scratch_shapes=[pltpu.SemaphoreType.DMA((2,))],
        compiler_params=PARAMS,
        cost_estimate=cost(0, depth, w.shape[1]),
    )(numbers, in_hbm(w), in_hbm(wq))


def first_product(rows, slabs):
    count = rows.shape[0]
    depth, cols = slabs[0].shape

    def kernel(rows_ref, slab_ref, slab_q_ref, full_ref, quant_ref, tail_ref):
        half = count // 2
        for part in range(2):
            here = slice(part * half, (part + 1) * half)
            x = rows_ref[here, :depth]
            full_ref[here, :] = jnp.dot(x, slab_ref[...], preferred_element_type=jnp.float32)
            quant_ref[here, :] = jnp.dot(x, slab_q_ref[...], preferred_element_type=jnp.float32)
        tail_ref[...] = rows_ref[:, depth:].astype(jnp.float32)

    return pl.pallas_call(
        kernel,
        in_specs=[VMEM_SPEC] * 3,
        out_specs=[VMEM_SPEC] * 3,
        out_shape=[pltpu.VMEM((count, cols), jnp.float32)] * 2 + [pltpu.VMEM((count, EXTRA), jnp.float32)],
        compiler_params=PARAMS,
        cost_estimate=cost(count, depth, cols),
    )(*[in_vmem(x) for x in (rows, *slabs)])


def fetching(numbers_ref, hbm_refs, slabs, sems, first):
    copies = []
    for n, slab in enumerate(slabs):
        copies.append(start_slab(numbers_ref[first + n // 2], hbm_refs[n % 2], slab, sems.at[n]))
    return copies


def add_product(numbers, w, wq, rows, depth, sums):
    count = rows[0].shape[0]
    cols = w.shape[1]
    quarters = len(rows)
    kept = 2 * quarters + 2

    def kernel(numbers_ref, w_ref, wq_ref, *refs):
        row_refs, ins, outs = refs[:quarters], refs[quarters : quarters + 3], refs[quarters + 3 : quarters + 6]
        slabs, sems = refs[quarters + 6 : -1], refs[-1]
        copies = fetching(numbers_ref, (w_ref, wq_ref), slabs, sems, 2)
        for q in range(quarters):
            for i in range(2):
                copies[2 * q + i].wait()
                before = outs[i][...] if q else ins[i][:count, :]
                outs[i][...] = before + jnp.dot(
                    row_refs[q][:, :depth], slabs[2 * q + i][...], preferred_element_type=jnp.float32
                )
        tail = ins[2][:count, :]
        for ref in row_refs:
            tail = tail + ref[:, depth:].astype(jnp.float32)
        outs[2][...] = tail
        for copy in copies[2 * quarters :]:
            copy.wait()

    out = pl.pallas_call(
        kernel,
        in_specs=[SMEM_SPEC, HBM_SPEC, HBM_SPEC] + [VMEM_SPEC] * (quarters + 3),
        out_specs=[VMEM_SPEC] * (3 + kept),
        out_shape=[pltpu.VMEM((count, cols), jnp.float32)] * 2
        + [pltpu.VMEM((count, EXTRA), jnp.float32)]
        + [pltpu.VMEM((depth, cols), w.dtype)] * kept,
        scratch_shapes=[pltpu.SemaphoreType.DMA((kept,))],
        compiler_params=PARAMS,
        cost_estimate=cost(count * quarters, depth, cols),
    )(numbers, in_hbm(w), in_hbm(wq), *[in_vmem(x) for x in (*rows, *sums)])
    return out[3:], out[:3]


def row_stats(expert, full, quant, total, extra):
    count = full.shape[0]
    diff = full - quant
    err = jnp.sum(diff * diff, axis=1, keepdims=True)
    power = jnp.sum(full * full, axis=1, keepdims=True)
    lane = lax.broadcasted_iota(jnp.int32, (count, EXTRA), 1)
    squares = total[:, 0:1] + total[:, 1:2] + total[:, 2:3]
    scale = lax.rsqrt(squares / D + epsilon)
    scale = scale * scale
    named = (lane >= 3) & (extra == expert.astype(jnp.float32))
    routed = jnp.sum(jnp.where(named, 1.0, 0.0), axis=1, keepdims=True)
    stats = jnp.where(lane == 0, err * (scale / FF), 0.0)
    stats = jnp.where(lane == 1, power * (scale / FF), stats)
    stats = jnp.where(lane == 2, routed, stats)
    stats = jnp.where(lane == 3, scale * routed, stats)
    return stats.T[:8, :]


def early_stats(numbers, rows, rest, slabs, sums, first_sums):
    count = rows.shape[0]
    done = sums[0].shape[0]
    depth, cols = slabs[0].shape
    quarters = len(rest)

    def kernel(numbers_ref, rows_ref, *refs):
        rest_refs, refs = refs[:quarters], refs[quarters:]
        slab_refs, ins, firsts, stats_ref = refs[: len(slabs)], refs[-7:-4], refs[-4:-1], refs[-1]
        expert = numbers_ref[0]
        here = slice(0, done)
        made = [
            before[...] + jnp.dot(rows_ref[here, :depth], slab[...], preferred_element_type=jnp.float32)
            for before, slab in zip(ins[:2], slab_refs[-2:])
        ]
        extra = rows_ref[here, depth:].astype(jnp.float32)
        stats_ref[:, here] = row_stats(expert, *made, ins[2][...] + extra, extra)
        here = slice(done, count)
        made = [
            before[here, :] + jnp.dot(rows_ref[here, :depth], slab[...], preferred_element_type=jnp.float32)
            for before, slab in zip(firsts[:2], slab_refs[-2:])
        ]
        extra = rows_ref[here, depth:].astype(jnp.float32)
        total = firsts[2][here, :] + extra
        for q, ref in enumerate(rest_refs):
            total = total + ref[:, depth:].astype(jnp.float32)
            for i in range(2):
                made[i] = made[i] + jnp.dot(
                    ref[:, :depth], slab_refs[2 * q + i][...], preferred_element_type=jnp.float32
                )
        stats_ref[:, here] = row_stats(expert, *made, total, extra)

    args = [rows, *rest, *slabs, *sums, *first_sums]
    return pl.pallas_call(
        kernel,
        in_specs=[SMEM_SPEC] + [VMEM_SPEC] * len(args),
        out_specs=VMEM_SPEC,
        out_shape=pltpu.VMEM((8, count), jnp.float32),
        compiler_params=PARAMS,
        cost_estimate=cost(count, depth, cols),
    )(numbers, *[in_vmem(x) for x in args])


def late_stats(numbers, rows, slabs, sums, early, tok, n_z):
    quarters = len(rows)
    count = rows[0].shape[0]
    depth, cols = slabs[0].shape

    def kernel(numbers_ref, *refs):
        row_refs, slab_refs = refs[:quarters], refs[quarters : 3 * quarters]
        full_ref, quant_ref, tail_ref, early_ref, stats_ref, out_ref = refs[3 * quarters :]
        expert = numbers_ref[0]
        core = expert % 2
        before = early_ref[...]
        here = slice(before.shape[1], before.shape[1] + count)
        total = tail_ref[here, :]
        made = [full_ref[here, :], quant_ref[here, :]]
        for q, ref in enumerate(row_refs):
            extra = ref[:, depth:].astype(jnp.float32)
            total = total + extra
            for i in range(2):
                made[i] = made[i] + jnp.dot(
                    ref[:, :depth], slab_refs[2 * q + i][...], preferred_element_type=jnp.float32
                )
        stats = row_stats(expert, *made, total, extra)
        stats_ref[...] = stats
        sums_early = jnp.sum(before * before[2:3, :], axis=1, keepdims=True)
        sums_here = sums_early + jnp.sum(stats * stats[2:3, :], axis=1, keepdims=True)
        lane = lax.broadcasted_iota(jnp.int32, (8, 2 * tok), 1)
        order = ((0, 0), (1, 1), (2, 4), (3, 5), (5, 3), (4, 2), (6, 6), (7, 7))
        for pair in range(4):
            both = stats if pair == 3 else before[:, pair * 2 * tok : (pair + 1) * 2 * tok]
            for odd in range(2):
                zero, one = order[2 * pair + odd]
                owner = expert ^ (zero + core * (one - zero))
                block = jnp.where(lane < tok, pltpu.roll(both, tok, 1) if odd else both, sums_here)
                for z in range(n_z):
                    out_ref[owner * n_z + z] = block[:2, :]

    return pl.pallas_call(
        kernel,
        in_specs=[SMEM_SPEC] + [VMEM_SPEC] * (3 * quarters + 4),
        out_specs=[VMEM_SPEC] * 2,
        out_shape=[
            pltpu.VMEM((8, count), jnp.float32),
            jax.ShapeDtypeStruct((8 * n_z, 2, 2 * tok), jnp.float32),
        ],
        compiler_params=PARAMS,
        cost_estimate=cost(count, depth, cols),
    )(numbers, *[in_vmem(x) for x in (*rows, *slabs, *sums, early)])


def hessian(rows, early, late, width):
    def kernel(rows_ref, early_ref, late_ref, out_ref):
        split = early_ref.shape[1]
        total = jnp.sum(early_ref[2:3, :], axis=1, keepdims=True) + jnp.sum(
            late_ref[2:3, :], axis=1, keepdims=True
        )
        weight_early = early_ref[...].T[:, 3:4]
        weight_late = late_ref[...].T[:, 3:4]
        step = 256
        for first in range(0, width, step):
            columns = slice(first, first + step)
            x = rows_ref[:split, columns].astype(jnp.float32)
            y = rows_ref[split:, columns].astype(jnp.float32)
            value = jnp.sum(x * x * weight_early, axis=0, keepdims=True)
            value = value + jnp.sum(y * y * weight_late, axis=0, keepdims=True)
            out_ref[:, columns] = 2.0 * value / total

    return pl.pallas_call(
        kernel,
        in_specs=[VMEM_SPEC] * 3,
        out_specs=VMEM_SPEC,
        out_shape=jax.ShapeDtypeStruct((1, width), jnp.float32),
        compiler_params=PARAMS,
        cost_estimate=pl.CostEstimate(flops=4 * rows.size, bytes_accessed=2 * rows.size, transcendentals=0),
    )(rows, in_vmem(early), in_vmem(late))


def finish(numbers, back, routes, weights, n_z):
    top, tok = routes.shape

    def kernel(numbers_ref, back_ref, routes_ref, weights_ref, token_ref, expert_ref):
        own = jnp.zeros((2, 2 * tok), jnp.float32)
        err = [jnp.zeros((1, tok), jnp.float32)] * top
        power = [jnp.zeros((1, tok), jnp.float32)] * top
        for i in range(back_ref.shape[0] // n_z):
            tile = back_ref[i * n_z]
            for z in range(1, n_z):
                tile = tile + back_ref[i * n_z + z]
            own = jnp.where(numbers_ref[0] == i, tile, own)
            for k in range(top):
                here = routes_ref[k : k + 1, :] == i
                err[k] = jnp.where(here, tile[0:1, :tok], err[k])
                power[k] = jnp.where(here, tile[1:2, :tok], power[k])
        total = jnp.zeros((1, tok), jnp.float32)
        for k in range(top):
            total = total + weights_ref[k : k + 1, :] * (err[k] / (power[k] + epsilon))
        token_ref[...] = total
        expert_ref[...] = own[0:1, tok : tok + 1] / (own[1:2, tok : tok + 1] + epsilon)

    return pl.pallas_call(
        kernel,
        in_specs=[SMEM_SPEC] + [VMEM_SPEC] * 3,
        out_specs=[VMEM_SPEC] * 2,
        out_shape=[jax.ShapeDtypeStruct((1, tok), jnp.float32), jax.ShapeDtypeStruct((1, 1), jnp.float32)],
    )(numbers, in_vmem(back), routes, weights)


def in_pieces(squares):
    high = lax.reduce_precision(squares, 8, 7)
    mid = lax.reduce_precision(squares - high, 8, 7)
    return [high, mid, squares - high - mid]


def line_device(residual, attn_parts, norm_gain, routes, route_weights, w_gate, w_gate_q):
    z = lax.axis_index("tensor")
    e = lax.axis_index("expert")
    n_z = 4
    tok = residual.shape[0]
    width = residual.shape[1]

    def over_z(x, k):
        return lax.ppermute(x, "tensor", [(i, i ^ k) for i in range(n_z)])

    def in_plane(x, zero, one):
        return lax.ppermute(x, "expert", [(i, i ^ (one if i & 1 else zero)) for i in range(8)])

    def quarter(k):
        return lax.dynamic_slice(attn_parts[0], (0, (z ^ k) * width), (tok, width))

    numbers = jnp.stack([e, z, z ^ 1, z ^ 2, z ^ 3]).astype(jnp.int32)
    w, wq = w_gate[0], w_gate_q[0]

    arrived = [over_z(quarter(k), k) for k in (3, 2, 1)]
    slabs = load_product(numbers, w, wq, width)
    residual, *slabs = lax.optimization_barrier((residual, *slabs))
    hidden = residual.astype(jnp.float32) + quarter(0).astype(jnp.float32)
    for part in arrived:
        hidden = hidden + part.astype(jnp.float32)
    squares = jnp.sum(hidden * hidden, axis=1, keepdims=True)
    own = (hidden * norm_gain.astype(jnp.float32)[None, :]).astype(jnp.bfloat16)
    extra = jnp.concatenate(
        in_pieces(squares)
        + [routes.astype(jnp.float32)]
        + [jnp.full((tok, EXTRA - 3 - routes.shape[1]), -1.0, jnp.float32)],
        axis=1,
    ).astype(jnp.bfloat16)
    own = jnp.concatenate([own, extra], axis=1)
    z_near, z_far = over_z(own, 1), over_z(own, 2)
    z_both = over_z(z_far, 1)

    def other_core(rows):
        return in_plane(rows, 1, 1)

    def next_chip(rows):
        return in_plane(rows, 2, 4)

    def opposite(rows):
        return in_plane(rows, 4, 2)

    def tied(x, *values):
        return lax.optimization_barrier((x, *values))[0]

    near = own, other_core(own)
    beside_x = next_chip(near[0])
    beside = beside_x, next_chip(tied(near[1], beside_x))
    across = opposite(beside[0])
    rows = jnp.concatenate([*near, *beside, *map(other_core, beside), across, other_core(across)], axis=0)
    first_sums = first_product(rows, slabs)
    across_far = over_z(across, 2)

    def of_quarters(parts):
        return [jnp.concatenate([x[q * tok : (q + 1) * tok] for x in parts], axis=0) for q in range(2)]

    pair = tied(jnp.concatenate([z_near, z_far], axis=0), *beside)
    near = pair, other_core(pair)
    beside = next_chip(near[0]), next_chip(near[1])
    across = opposite(tied(beside[0], beside[1], *first_sums))
    ready = of_quarters((*near, *beside))
    ready[0] = tied(ready[0], z_both)
    slabs, sums = add_product(numbers, w, wq, ready, width, first_sums)
    rest = of_quarters([other_core(x) for x in beside])
    last = of_quarters((across, other_core(tied(across, *sums))))

    single = tied(z_both, beside[1])
    across_far = tied(across_far, beside[1], *first_sums)
    near = single, other_core(single)
    beside = next_chip(near[0]), next_chip(near[1])
    across = over_z(across_far, 1)
    most = jnp.concatenate([*near, *beside, *map(other_core, beside)], axis=0)
    early = early_stats(numbers, most, rest, slabs, sums, first_sums)
    last.append(jnp.concatenate([across, other_core(across)], axis=0))
    late, payload = late_stats(numbers, last, slabs, first_sums, early, tok, n_z)

    back = lax.all_to_all(payload, ("expert", "tensor"), split_axis=0, concat_axis=0, tiled=True)
    hess = hessian(rows, early, late, width)
    token_error, expert_total = finish(numbers, back, routes.T, route_weights.T, n_z)
    return (token_error.reshape(tok), expert_total.reshape(1), hess.reshape(1, width))


def solution(mesh):
    placed = (
        P("expert", "tensor"),
        P("tensor", "expert", None),
        P("tensor"),
        P("expert", None),
        P("expert", None),
        P("expert", None, "tensor"),
        P("expert", None, "tensor"),
    )
    on_line = mesh.shape["expert"] == 8 and mesh.shape["tensor"] == 4
    return jax.shard_map(
        line_device if on_line else general_device,
        mesh=mesh,
        in_specs=placed,
        out_specs=(P("expert"), P("expert"), P("expert", "tensor")),
        check_vma=False,
    )
```
